32 devices in a mesh: groups: 1, sec: 32 (over z, y, x, core).
Axes of the slice: x: 2, y: 2, z: 4, core: 2. Of those that a mesh axis runs over, the one named last changes fastest.
Arguments:
- wavefunction: bfloat16 [32, 192, 192], P(('groups', 'sec')), may hold values from -6 to 6
- left_environment: bfloat16 [192, 192, 768], P(('groups', 'sec'))
- right_environment: bfloat16 [192, 192, 768], P(('groups', 'sec'))
- sector_sizes: int32 [2, 2], P(None, 'groups'), may hold values from 64 to 768, as said below
- pairing: int32 [2], P('groups'), may hold values from 0 to 1, each once
- term_mask: int32 [2, 24], P('groups'), may hold values 0 or 1
- coupling: int32 [2, 24], P('groups'), may hold values from 0 to 1
Outputs:
- first_image: bfloat16 [32, 192, 192], P(('groups', 'sec'))
- second_image: bfloat16 [32, 192, 192], P(('groups', 'sec'))
The draws below stay inside these ranges and needn't reach their ends.
Inputs may be any that keep to these rules, and one draw needn't show every extreme that they name: `sector_sizes`: each row reaches 768. `pairing`: A permutation of the sectors.
All inputs are finite; a program needn't handle non-finite values.
Results may differ from the reference program's by a relative error of at most 0.007.
Values may be sent and summed in bfloat16 or wider, within the bound.
No kernel may reach another device: no remote copies, remote signals or barrier semaphores. Data moves between devices by JAX's collectives and lax.ppermute only.
A program may use at most 128 MiB of HBM per device.

```python
import jax
import jax.numpy as jnp
from jax import lax

CAPACITY = 768
TERMS = 24
GRID_ROWS = 4
GRID_COLS = 4
SECTORS = 2
TILE_ROWS = 192
TILE_COLS = 192
TERMS_DEV = 6
N_SEC = 32


def environment_values(noise_draw, rough_key, level_key, lowest, highest):
    slot_count = noise_draw.shape[0]
    term_levels = jnp.exp(jax.random.uniform(level_key, (SECTORS * TERMS,), jnp.float32, jnp.log(lowest), jnp.log(highest)))
    slot_line = jnp.arange(slot_count, dtype=jnp.int32)
    block_of = slot_line // (GRID_ROWS * GRID_COLS * TERMS_DEV)
    term_of = slot_line // TERMS_DEV % GRID_COLS * TERMS_DEV + slot_line % TERMS_DEV
    slot_level = jnp.take(term_levels, (block_of * TERMS + term_of).astype(jnp.int32))
    slot_ids = jax.lax.broadcasted_iota(jnp.int32, noise_draw.shape, 0)
    row_ids = jax.lax.broadcasted_iota(jnp.int32, noise_draw.shape, 1)
    col_ids = jax.lax.broadcasted_iota(jnp.int32, noise_draw.shape, 2)
    row_group = slot_ids // TERMS_DEV // GRID_COLS % GRID_ROWS
    on_diagonal = row_group * TILE_ROWS + row_ids == col_ids
    roughness = jax.random.uniform(rough_key, noise_draw.shape[:2], jnp.float32, 0.6, 1.4)
    diagonal = slot_level[:, None] * roughness
    noise_scale = CAPACITY ** (-0.5) * TERMS ** (-0.25)
    return noise_draw * noise_scale + jnp.where(on_diagonal, diagonal[:, :, None], 0.0)


def draw_left_environment(key, part):
    key = jax.random.fold_in(key, 11)
    noise_key, rough_key, level_key = jax.random.split(key, 3)
    shape_dims = (N_SEC * TERMS_DEV, TILE_ROWS, CAPACITY)
    noise_draw = jax.random.normal(noise_key, shape_dims, jnp.float32)
    values = environment_values(noise_draw, rough_key, level_key, 0.1, 0.9)
    return values.astype(jnp.bfloat16)


def draw_right_environment(key, part):
    key = jax.random.fold_in(key, 12)
    noise_key, rough_key, level_key = jax.random.split(key, 3)
    shape_dims = (N_SEC * TERMS_DEV, TILE_ROWS, CAPACITY)
    noise_draw = jax.random.normal(noise_key, shape_dims, jnp.float32)
    values = environment_values(noise_draw, rough_key, level_key, 0.1, 0.9)
    return values.astype(jnp.bfloat16)


def draw_sector_sizes(key, part):
    key = jax.random.fold_in(key, 13)
    size_key, place_key = jax.random.split(key)
    lowest = min(64, CAPACITY // 4)
    drawn_sizes = jax.random.randint(size_key, (2, SECTORS), lowest, CAPACITY + 1)
    largest_at = jax.random.randint(place_key, (2, 1), 0, SECTORS)
    placed = jnp.arange(SECTORS, dtype=jnp.int32)[None, :] == largest_at
    return jnp.where(placed, CAPACITY, drawn_sizes).astype(jnp.int32)


def place_ends(array, rng, smallest, largest):
    spot = [jax.random.randint(jax.random.fold_in(rng, axis), (), 0, length) for axis, length in enumerate(array.shape)]
    widest = array.shape.index(max(array.shape))
    beside = spot[:widest] + [(spot[widest] + 1) % array.shape[widest]] + spot[widest + 1:]
    return array.at[tuple(spot)].set(smallest).at[tuple(beside)].set(largest)


def level_of(key, extent, cuts, least, top_value):
    level = 1.0
    for position, shards_of in cuts:
        heights = jax.random.uniform(jax.random.fold_in(jax.random.fold_in(key, 6), position), (shards_of,), jnp.float32, least / len(cuts), top_value / len(cuts))
        level = level * jnp.repeat(jnp.exp(heights), extent[position] // shards_of).reshape((-1,) + (1,) * (len(extent) - 1 - position))
    return level


def gaussian(key, extent, deviation, limit, pieces=(), kind=jnp.bfloat16):
    drawn = jax.random.normal(key, extent, jnp.float32) * deviation
    if len(pieces) > 0:
        drawn = level_of(key, extent, pieces, -0.22, 0.18) * drawn
    return jnp.clip(drawn, min=-limit, max=limit).astype(kind)


def setup_inputs(seed: int = 0, part: int = 0) -> dict:
    key_of = jax.random.split(jax.random.key(seed), 8)
    part_keys = jax.random.split(jax.random.fold_in(key_of[7], part), 8)
    wavefunction = gaussian(part_keys[0], (N_SEC, TILE_ROWS, TILE_COLS), 1.0, 6.0, ((0, 32),))
    left_environment = draw_left_environment(jax.random.fold_in(jax.random.fold_in(key_of[7], part), 71), part)
    right_environment = draw_right_environment(jax.random.fold_in(jax.random.fold_in(key_of[7], part), 71), part)
    sector_sizes = draw_sector_sizes(jax.random.fold_in(jax.random.fold_in(key_of[7], part), 71), part)
    pairing = jax.random.permutation(part_keys[4], SECTORS).astype(jnp.int32)
    term_mask = place_ends((jax.random.randint(part_keys[5], (SECTORS, TERMS), 0, 4) < 3).astype(jnp.int32), jax.random.fold_in(part_keys[5], 1), 0, 1)
    coupling = place_ends(jax.random.randint(part_keys[6], (SECTORS, TERMS), 0, SECTORS), jax.random.fold_in(part_keys[6], 1), 0, SECTORS - 1).astype(jnp.int32)
    return {"wavefunction": wavefunction, "left_environment": left_environment, "right_environment": right_environment, "sector_sizes": sector_sizes, "pairing": pairing, "term_mask": term_mask, "coupling": coupling}


EPSILON = 1e-06

def to_blocks(tiles):
    shaped = tiles.reshape(SECTORS, GRID_ROWS, GRID_COLS, TILE_ROWS, TILE_COLS)
    return shaped.transpose(0, 1, 3, 2, 4).reshape(SECTORS, CAPACITY, CAPACITY)

def from_blocks(blocks):
    shaped = blocks.reshape(SECTORS, GRID_ROWS, TILE_ROWS, GRID_COLS, TILE_COLS)
    return shaped.transpose(0, 1, 3, 2, 4).reshape(N_SEC, TILE_ROWS, TILE_COLS)

def to_terms(environment):
    shaped = environment.reshape(SECTORS, GRID_ROWS, GRID_COLS, TERMS_DEV, TILE_ROWS, CAPACITY)
    return shaped.transpose(0, 2, 3, 1, 4, 5).reshape(SECTORS, TERMS, CAPACITY, CAPACITY)

def apply_operator(blocks, lefts, rights, active, live_masks, coupling):

    def one_sector(items):
        left_terms, right_terms, weights, live_mask, sources = items
        source_blocks = jnp.take(blocks, sources.astype(jnp.int32), axis=0).astype(jnp.float32)
        mixed_terms = jnp.einsum('wrc,wcs->wrs', left_terms.astype(jnp.float32), source_blocks)
        mixed_terms = (mixed_terms * weights[:, None, None]).astype(jnp.bfloat16)
        image = jnp.einsum('wrs,wst->rt', mixed_terms.astype(jnp.float32), right_terms.astype(jnp.float32))
        return (image * live_mask).astype(jnp.bfloat16)
    return lax.map(one_sector, (lefts, rights, active, live_masks, coupling))

def reference(wavefunction, left_environment, right_environment, sector_sizes, pairing, term_mask, coupling):
    positions = jnp.arange(CAPACITY, dtype=jnp.int32)
    left_sizes = sector_sizes[0]
    right_sizes = sector_sizes[1][pairing]
    row_live = (positions[None, :] < left_sizes[:, None]).astype(jnp.float32)
    col_live = (positions[None, :] < right_sizes[:, None]).astype(jnp.float32)
    live_masks = row_live[:, :, None] * col_live[:, None, :]
    lefts = to_terms(left_environment)
    rights = to_terms(right_environment)
    active = term_mask.astype(jnp.float32)
    start_blocks = (to_blocks(wavefunction).astype(jnp.float32) * live_masks).astype(jnp.bfloat16)
    first_blocks = apply_operator(start_blocks, lefts, rights, active, live_masks, coupling)
    start_value = start_blocks.astype(jnp.float32)
    first_value = first_blocks.astype(jnp.float32)
    square = jnp.sum(start_value * start_value)
    quotient = jnp.sum(start_value * first_value) / square
    residual = first_value - quotient * start_value
    residual_square = jnp.sum(residual * residual)
    second_input = (residual * lax.rsqrt(residual_square / square + EPSILON)).astype(jnp.bfloat16)
    second_blocks = apply_operator(second_input, lefts, rights, active, live_masks, coupling)
    return (from_blocks(first_blocks), from_blocks(second_blocks))
```

```python
import jax
import jax.numpy as jnp
from jax import lax
from jax.experimental import pallas as pl
from jax.experimental.pallas import tpu as pltpu
from jax.sharding import PartitionSpec as P

GRID_ROWS = 4
GRID_COLS = 4
CORE, XBIT, YBIT, ZBIT = 1, 2, 4, 8
SECTOR_BIT = GRID_ROWS * GRID_COLS
EPSILON = 1e-06
SCALAR_ROWS = 16


def exchange(block, flip):
    count = lax.axis_size("sec")
    return lax.ppermute(block, "sec", [(i, i ^ flip) for i in range(count)])


def swap_xz(block):
    count = lax.axis_size("sec")
    route = []
    for i in range(count):
        x, z = i // XBIT % 2, i // ZBIT % 2
        route.append((i, i - x * XBIT - z * ZBIT + z * XBIT + x * ZBIT))
    return lax.ppermute(block, "sec", route)


def place():
    index = lax.axis_index("sec")
    return index % 2, index // XBIT % 2, index // YBIT % 2, index // ZBIT % 2, index // SECTOR_BIT


def smem():
    return pl.BlockSpec(memory_space=pltpu.SMEM)


def vmem():
    return pl.BlockSpec(memory_space=pltpu.VMEM)


def live_block(sizes, row_start, col_start, shape):
    rows = row_start + lax.broadcasted_iota(jnp.int32, shape, 0)
    cols = col_start + lax.broadcasted_iota(jnp.int32, shape, 1)
    return (rows < sizes[0]) & (cols < sizes[1])


def sizes_of(sizes_ref, pairing_ref, sector):
    return sizes_ref[0, sector], sizes_ref[1, pairing_ref[sector]]


def start_kernel(index_ref, sizes_ref, pairing_ref, wave_ref, out_ref):
    index = index_ref[0]
    sector = index // SECTOR_BIT
    rows, cols = out_ref.shape
    keep = live_block(
        sizes_of(sizes_ref, pairing_ref, sector),
        index // GRID_COLS % GRID_ROWS * rows,
        index % GRID_COLS * cols,
        (rows, cols),
    )
    out_ref[...] = jnp.where(keep, wave_ref[0].astype(jnp.float32), 0.0).astype(jnp.bfloat16)


def copies_in(index, refs, scratch, sems, count):
    left_own, left_peer, right_own, right_peer = refs
    lefts, rights = scratch
    tile = left_own.shape[1]
    y, z = index // YBIT % 2, index // ZBIT % 2
    found = []
    for k in range(count):
        found.append(
            [
                pltpu.make_async_copy(left_own.at[k], lefts.at[k, pl.ds(z * tile, tile)], sems.at[k, 0]),
                pltpu.make_async_copy(
                    left_peer.at[k], lefts.at[k, pl.ds((1 - z) * tile, tile)], sems.at[k, 1]
                ),
                pltpu.make_async_copy(
                    right_own.at[k], rights.at[pl.ds(k * 2 * tile + y * tile, tile)], sems.at[k, 2]
                ),
                pltpu.make_async_copy(
                    right_peer.at[k], rights.at[pl.ds(k * 2 * tile + (1 - y) * tile, tile)], sems.at[k, 3]
                ),
            ]
        )
    return found


def apply_terms(index, first_term, mask_ref, coupling_ref, vector, lefts, rights, mixed, copies):
    sector = index // SECTOR_BIT
    group = index % GRID_COLS
    count, height, _ = lefts.shape
    width = vector.shape[2]
    terms = mask_ref.shape[1] // GRID_COLS
    for k in range(count):
        term = group * terms + first_term + k
        for copy in copies[k]:
            copy.wait()
        source = coupling_ref[sector, term]
        product = jnp.dot(lefts[k], vector[source], preferred_element_type=jnp.float32)
        weight = mask_ref[sector, term].astype(jnp.float32)
        mixed[:, k * width : (k + 1) * width] = (product * weight).astype(jnp.bfloat16)
    return jnp.dot(mixed[...], rights[...], preferred_element_type=jnp.float32)


def first_kernel(
    first_term,
    last,
    index_ref,
    mask_ref,
    coupling_ref,
    pieces_ref,
    left_own,
    left_peer,
    right_own,
    right_peer,
    *rest,
):
    index = index_ref[0]
    rest = list(rest)
    before = rest.pop(0) if first_term else None
    if last:
        kept_ref, sent_ref = rest[:2]
        rest = rest[2:]
    else:
        total_ref = rest[0]
        rest = rest[1:]
    vector, lefts, rights, mixed, sems = rest
    count, height, _ = lefts.shape
    tile = height // 2
    copies = copies_in(index, (left_own, left_peer, right_own, right_peer), (lefts, rights), sems, count)
    for group in copies:
        for copy in group:
            copy.start()
    core, x, y = index % 2, index // XBIT % 2, index // YBIT % 2
    sector = index // SECTOR_BIT
    for xr in range(2):
        for yr in range(2):
            for sr in range(vector.shape[0]):
                row = (2 * (x ^ xr) + (y ^ yr)) * tile
                vector[sector ^ sr, pl.ds(pl.multiple_of(row, 64), tile), :] = pieces_ref[xr, yr, sr]
    total = apply_terms(index, first_term, mask_ref, coupling_ref, vector, lefts, rights, mixed, copies)
    if before is not None:
        total = total + before[...]
    if not last:
        total_ref[...] = total
    else:

        @pl.when(core == 0)
        def _():
            kept_ref[...] = total[:tile]
            sent_ref[...] = total[tile:].astype(jnp.bfloat16)

        @pl.when(core == 1)
        def _():
            kept_ref[...] = total[tile:]
            sent_ref[...] = total[:tile].astype(jnp.bfloat16)


def split_kernel(index_ref, kept_ref, got_ref, own_ref, to_x, to_z, to_xz):
    index = index_ref[0]
    x, z = index // XBIT % 2, index // ZBIT % 2
    rows, cols = own_ref.shape

    def part(row_half, col_half):
        at = (
            pl.ds(pl.multiple_of(row_half * rows, 32), rows),
            pl.ds(pl.multiple_of(col_half * cols, 128), cols),
        )
        return kept_ref[at] + got_ref[at].astype(jnp.float32)

    own_ref[...] = part(x, z)
    to_x[...] = part(1 - x, z).astype(jnp.bfloat16)
    to_z[...] = part(x, 1 - z).astype(jnp.bfloat16)
    to_xz[...] = part(1 - x, 1 - z).astype(jnp.bfloat16)


def join_kernel(index_ref, sizes_ref, pairing_ref, own_ref, from_x, from_z, from_xz, out_ref):
    index = index_ref[0]
    core, x, y, z = index % 2, index // XBIT % 2, index // YBIT % 2, index // ZBIT % 2
    rows, cols = out_ref.shape
    total = own_ref[...] + from_x[...].astype(jnp.float32)
    total += from_z[...].astype(jnp.float32) + from_xz[...].astype(jnp.float32)
    keep = live_block(
        sizes_of(sizes_ref, pairing_ref, index // SECTOR_BIT),
        (2 * core + y) * 2 * rows + x * rows,
        z * cols,
        (rows, cols),
    )
    out_ref[...] = jnp.where(keep, total, 0.0).astype(jnp.bfloat16)


def second_kernel(
    index_ref,
    mask_ref,
    coupling_ref,
    start_ref,
    pieces_own,
    pieces_peer,
    left_own,
    left_peer,
    right_own,
    right_peer,
    kept_ref,
    sent_ref,
    tile_ref,
    sums_ref,
    vector,
    lefts,
    rights,
    mixed,
    sems,
):
    index = index_ref[0]
    count, height, _ = lefts.shape
    tile = height // 2
    half = tile // 2
    copies = copies_in(index, (left_own, left_peer, right_own, right_peer), (lefts, rights), sems, count)
    for group in copies:
        for copy in group:
            copy.start()
    core, x, y = index % 2, index // XBIT % 2, index // YBIT % 2
    sector = index // SECTOR_BIT
    sectors = vector.shape[0]
    for pieces, z_row in ((pieces_own, core), (pieces_peer, 1 - core)):
        for xr in range(2):
            for yr in range(2):
                for sr in range(sectors):
                    row = (2 * z_row + (y ^ yr)) * tile + (x ^ xr) * half
                    vector[sector ^ sr, pl.ds(pl.multiple_of(row, 32), half), :] = pieces[2 * xr + yr, sr]
    square = jnp.zeros((8, vector.shape[2]), jnp.float32)
    inner, norm = square, square
    for xr in range(2):
        for yr in range(2):
            for sr in range(sectors):
                row = (2 * (x ^ xr) + (y ^ yr)) * tile
                image = vector[sector ^ sr, pl.ds(pl.multiple_of(row, 64), tile), :].astype(jnp.float32)
                start = start_ref[xr, yr, sr].astype(jnp.float32)
                image = image.reshape(tile // 8, 8, -1)
                start = start.reshape(tile // 8, 8, -1)
                square += jnp.sum(start * start, axis=0)
                inner += jnp.sum(start * image, axis=0)
                norm += jnp.sum(image * image, axis=0)
    for k, sums in enumerate((square, inner, norm)):
        sums_ref[8 * k : 8 * (k + 1), :] = jnp.broadcast_to(jnp.sum(sums), (8, sums_ref.shape[1]))
    total = apply_terms(index, 0, mask_ref, coupling_ref, vector, lefts, rights, mixed, copies)
    image_tile = vector[sector, pl.ds(pl.multiple_of((2 * x + y) * tile, 64), tile), :]

    def give(mine, other):
        for col_half in range(2):
            base = col_half * 2 * tile
            kept_ref[col_half] = total[:, base + mine * tile : base + (mine + 1) * tile]
            sent_ref[col_half] = total[:, base + other * tile : base + (other + 1) * tile].astype(
                jnp.bfloat16
            )
        tile_ref[...] = image_tile[:, mine * tile : (mine + 1) * tile]

    @pl.when(core == 0)
    def _():
        give(0, 1)

    @pl.when(core == 1)
    def _():
        give(1, 0)


def last_split_kernel(index_ref, kept_ref, got_ref, sums_ref, own_ref, to_x, to_z, to_xz):
    index = index_ref[0]
    x, z = index // XBIT % 2, index // ZBIT % 2
    rows, cols = own_ref.shape

    def part(row_half, col_half):
        at = (col_half, pl.ds(pl.multiple_of(row_half * rows, 64), rows))
        return kept_ref[at] + got_ref[at].astype(jnp.float32)

    own_ref[...] = part(z, x)
    to_x[...] = part(z, 1 - x).astype(jnp.bfloat16)
    to_z[:rows, :] = part(1 - z, x).astype(jnp.bfloat16)
    to_xz[...] = part(1 - z, 1 - x).astype(jnp.bfloat16)
    for k in range(3):
        value = jnp.broadcast_to(sums_ref[8 * k : 8 * k + 1, :cols], (SCALAR_ROWS, cols))
        for level in range(3):
            piece = value.astype(jnp.bfloat16)
            to_z[pl.ds(rows + (3 * k + level) * SCALAR_ROWS, SCALAR_ROWS), :] = piece
            value = value - piece.astype(jnp.float32)


def last_join_kernel(
    index_ref, sizes_ref, pairing_ref, own_ref, from_x, from_z, from_xz, sums_ref, image_ref, out_ref
):
    index = index_ref[0]
    _, rows, cols = out_ref.shape
    total = own_ref[...] + from_x[...].astype(jnp.float32)
    total += from_z[:rows, :].astype(jnp.float32) + from_xz[...].astype(jnp.float32)
    sums = []
    for k in range(3):
        value = sums_ref[8 * k : 8 * k + 1, :cols]
        for level in range(3):
            at = rows + (3 * k + level) * SCALAR_ROWS
            value = value + from_z[at : at + SCALAR_ROWS, :].astype(jnp.float32)[:1]
        sums.append(value)
    square, inner, norm = sums
    quotient = inner / square
    residual_square = norm - quotient * inner
    scale = lax.rsqrt(jnp.maximum(residual_square, 0.0) / square + EPSILON)
    keep = live_block(
        sizes_of(sizes_ref, pairing_ref, index // SECTOR_BIT),
        index // GRID_COLS % GRID_ROWS * rows,
        index % GRID_COLS * cols,
        (rows, cols),
    )
    second = (total - quotient * image_ref[...].astype(jnp.float32)) * scale
    out_ref[0] = jnp.where(keep, second, 0.0).astype(jnp.bfloat16)


def on_device(
    wavefunction, left_environment, right_environment, sector_sizes, pairing, term_mask, coupling
):
    tile = wavefunction.shape[1]
    terms = left_environment.shape[0]
    sectors = lax.axis_size("sec") // SECTOR_BIT
    capacity = tile * GRID_ROWS
    bf16, f32 = jnp.bfloat16, jnp.float32
    index = lax.axis_index("sec").astype(jnp.int32)[None]
    core = index[0] % 2
    limit = pltpu.CompilerParams(vmem_limit_bytes=40 * 2**20)
    anywhere = pl.BlockSpec(memory_space=pl.ANY)

    def shaped(*shape, dtype=bf16):
        return jax.ShapeDtypeStruct(shape, dtype)

    left_peer, right_peer = [], []
    chunks = ((0, terms // 2), (terms // 2, terms))
    for low, high in chunks:
        left_peer.append(exchange(left_environment[low:high], ZBIT))
        right_peer.append(exchange(right_environment[low:high], YBIT))

    start_tile = pl.pallas_call(
        start_kernel,
        out_shape=shaped(tile, tile),
        in_specs=[smem(), smem(), smem(), vmem()],
        out_specs=vmem(),
    )(index, sector_sizes, pairing, wavefunction)

    def sector_pieces(piece):
        gathered = piece[None]
        flip = SECTOR_BIT
        while flip < lax.axis_size("sec"):
            gathered = jnp.concatenate([gathered, exchange(gathered, flip)])
            flip *= 2
        return gathered

    pieces = sector_pieces(swap_xz(start_tile))
    pieces = jnp.stack([pieces, exchange(pieces, YBIT)])
    pieces = jnp.stack([pieces, exchange(pieces, XBIT)])
    peer = exchange(pieces, CORE)
    start_pieces = jnp.where(
        core == 0, jnp.concatenate([pieces, peer], -1), jnp.concatenate([peer, pieces], -1)
    )

    def scratch(count):
        return [
            pltpu.VMEM((sectors, capacity, 2 * tile), bf16),
            pltpu.VMEM((count, 2 * tile, capacity), bf16),
            pltpu.VMEM((count * 2 * tile, capacity), bf16),
            pltpu.VMEM((2 * tile, count * 2 * tile), bf16),
            pltpu.SemaphoreType.DMA((count, 4)),
        ]

    def work(count):
        macs = count * 2 * tile * capacity * 2 * tile * 2
        return pl.CostEstimate(
            flops=2 * macs, bytes_accessed=count * 4 * tile * capacity * 2, transcendentals=0
        )

    total = None
    for number, (low, high) in enumerate(chunks):
        last = high == terms
        count = high - low
        extra = [] if total is None else [total]
        total = pl.pallas_call(
            lambda *refs, low=low, last=last: first_kernel(low, last, *refs),
            out_shape=(
                [shaped(tile, capacity, dtype=f32), shaped(tile, capacity)]
                if last
                else shaped(2 * tile, capacity, dtype=f32)
            ),
            in_specs=[smem()] * 3 + [vmem()] + [anywhere] * 4 + [vmem()] * len(extra),
            out_specs=[vmem(), vmem()] if last else vmem(),
            scratch_shapes=scratch(count),
            compiler_params=limit,
            cost_estimate=work(count),
        )(
            index,
            term_mask,
            coupling,
            start_pieces,
            left_environment[low:high],
            left_peer[number],
            right_environment[low:high],
            right_peer[number],
            *extra,
        )
    kept, sent = total
    got = exchange(sent, CORE)
    unit = (tile // 2, 2 * tile)
    own, to_x, to_z, to_xz = pl.pallas_call(
        split_kernel,
        out_shape=[shaped(*unit, dtype=f32)] + [shaped(*unit)] * 3,
        in_specs=[smem(), vmem(), vmem()],
        out_specs=[vmem()] * 4,
    )(index, kept, got)
    image_unit = pl.pallas_call(
        join_kernel,
        out_shape=shaped(*unit),
        in_specs=[smem()] * 3 + [vmem()] * 4,
        out_specs=vmem(),
    )(
        index,
        sector_sizes,
        pairing,
        own,
        exchange(to_x, XBIT),
        exchange(to_z, ZBIT),
        exchange(to_xz, XBIT | ZBIT),
    )

    units = sector_pieces(image_unit)
    units = jnp.stack(
        [units, exchange(units, YBIT), exchange(units, XBIT), exchange(units, XBIT | YBIT)]
    )
    units_peer = exchange(units, CORE)
    kept, sent, image_tile, sums = pl.pallas_call(
        second_kernel,
        out_shape=[
            shaped(2, 2 * tile, tile, dtype=f32),
            shaped(2, 2 * tile, tile),
            shaped(tile, tile),
            shaped(24, 2 * 128, dtype=f32),
        ],
        in_specs=[smem()] * 3 + [vmem()] * 3 + [anywhere] * 4,
        out_specs=[vmem()] * 4,
        scratch_shapes=scratch(terms),
        compiler_params=limit,
        cost_estimate=work(terms),
    )(
        index,
        term_mask,
        coupling,
        start_pieces,
        units,
        units_peer,
        left_environment,
        jnp.concatenate(left_peer),
        right_environment,
        jnp.concatenate(right_peer),
    )
    got = exchange(sent, CORE)
    first_tile = swap_xz(image_tile)
    own, to_x, to_z, to_xz = pl.pallas_call(
        last_split_kernel,
        out_shape=[
            shaped(tile, tile, dtype=f32),
            shaped(tile, tile),
            shaped(tile + 9 * SCALAR_ROWS, tile),
            shaped(tile, tile),
        ],
        in_specs=[smem()] + [vmem()] * 3,
        out_specs=[vmem()] * 4,
    )(index, kept, got, sums)
    second = pl.pallas_call(
        last_join_kernel,
        out_shape=shaped(1, tile, tile),
        in_specs=[smem()] * 3 + [vmem()] * 6,
        out_specs=vmem(),
    )(
        index,
        sector_sizes,
        pairing,
        own,
        exchange(to_x, XBIT),
        exchange(to_z, ZBIT),
        exchange(to_xz, XBIT | ZBIT),
        sums,
        first_tile,
    )
    return first_tile[None], second


def solution(mesh):
    return jax.shard_map(
        on_device,
        mesh=mesh,
        in_specs=(
            P(("groups", "sec"), None, None),
            P(("groups", "sec"), None, None),
            P(("groups", "sec"), None, None),
            P(None, "groups"),
            P("groups"),
            P("groups", None),
            P("groups", None),
        ),
        out_specs=(P(("groups", "sec"), None, None), P(("groups", "sec"), None, None)),
        check_vma=False,
    )
```

```python
import jax
import jax.numpy as jnp
from jax import lax
from jax.experimental import pallas as pl
from jax.experimental.pallas import tpu as pltpu
from jax.sharding import PartitionSpec as P

GRID_ROWS = 4
GRID_COLS = 4
CORE, XBIT, YBIT, ZBIT = 1, 2, 4, 8
SECTOR_BIT = GRID_ROWS * GRID_COLS
EPSILON = 1e-06
EXTRA_ROWS = 16
MIB = 2**20
PLAN_BITS = 5


def exchange(block, flip, swapped=False):
    route = []
    for i in range(lax.axis_size("sec")):
        x, z = i // XBIT % 2, i // ZBIT % 2
        moved = i - x * XBIT - z * ZBIT + z * XBIT + x * ZBIT if swapped else i
        route.append((i, moved ^ flip))
    return lax.ppermute(block, "sec", route)


def smem():
    return pl.BlockSpec(memory_space=pltpu.SMEM)


def vmem():
    return pl.BlockSpec(memory_space=pltpu.VMEM)


def anywhere():
    return pl.BlockSpec(memory_space=pl.ANY)


def live_block(sizes, row_start, col_start, shape):
    rows = row_start + lax.broadcasted_iota(jnp.int32, shape, 0)
    cols = col_start + lax.broadcasted_iota(jnp.int32, shape, 1)
    return (rows < sizes[0]) & (cols < sizes[1])


def place_copies(sources, target, places, sems):
    tile = sources[0].shape[1]
    found = []
    for k in range(sources[0].shape[0]):
        pair = []
        for slot in range(2):
            row = pl.multiple_of(places[slot] * tile, tile)
            copy = pltpu.make_async_copy(
                sources[slot].at[k], target.at[k, pl.ds(row, tile)], sems.at[k, slot]
            )
            copy.start()
            pair.append(copy)
        found.append(pair)
    return found


def term_of(plan, sectors, terms, k):
    base = PLAN_BITS + 2 * sectors
    return plan[base + k], plan[base + terms + k].astype(jnp.float32)


def mix(plan, sectors, terms, k, left, vector):
    source, weight = term_of(plan, sectors, terms, k)
    product = jnp.dot(left, vector[source], preferred_element_type=jnp.float32)
    return (product * weight).astype(jnp.bfloat16)


def start_kernel(sectors, plan, near, far, left_own, vector, mixed_ref, square_ref, lefts, sems):
    terms, tile, _ = left_own.shape
    width = 2 * tile
    copies = []
    for k in range(terms):
        copy = pltpu.make_async_copy(left_own.at[k], lefts.at[k], sems.at[k])
        copy.start()
        copies.append(copy)
    core, x, y, z = plan[0], plan[1], plan[2], plan[3]
    square = jnp.zeros((8, width), jnp.float32)
    for xr in range(2):
        for yr in range(2):
            for sr in range(sectors):
                sector = plan[4] ^ sr
                row = (2 * (x ^ xr) + (y ^ yr)) * tile
                sizes = plan[PLAN_BITS + 2 * sector], plan[PLAN_BITS + 2 * sector + 1]
                mine, other = near[xr, yr, sr], far[xr, yr, sr]
                low = jnp.where(core == 0, mine, other).astype(jnp.float32)
                high = jnp.where(core == 0, other, mine).astype(jnp.float32)
                both = jnp.concatenate([low, high], axis=1)
                both = jnp.where(live_block(sizes, row, z * width, both.shape), both, 0.0)
                square += jnp.sum((both * both).reshape(tile // 8, 8, width), axis=0)
                at = pl.ds(pl.multiple_of(row, tile), tile)
                vector[sector, at, :] = both.astype(jnp.bfloat16)
    square_ref[...] = jnp.broadcast_to(jnp.sum(square), square_ref.shape)
    for k in range(terms):
        copies[k].wait()
        mixed_ref[:, k * width : (k + 1) * width] = mix(plan, sectors, terms, k, lefts[k], vector)


def first_kernel(
    sectors,
    plan,
    vector,
    mixed_own,
    left_peer,
    right_own,
    right_peer,
    kept_ref,
    sent_ref,
    lefts,
    rights,
    mixed,
    left_sems,
    right_sems,
):
    terms, tile, _ = left_peer.shape
    width = 2 * tile
    left_copies = []
    for k in range(terms):
        copy = pltpu.make_async_copy(left_peer.at[k], lefts.at[k], left_sems.at[k])
        copy.start()
        left_copies.append(copy)
    core, x, y, z = plan[0], plan[1], plan[2], plan[3]
    right_copies = place_copies((right_own, right_peer), rights, (y, 1 - y), right_sems)
    own = pl.ds(pl.multiple_of(z * tile, tile), tile)
    peer = pl.ds(pl.multiple_of((1 - z) * tile, tile), tile)
    mixed[own, :] = mixed_own[...]
    for k in range(terms):
        left_copies[k].wait()
        mixed[peer, k * width : (k + 1) * width] = mix(plan, sectors, terms, k, lefts[k], vector)
    total = collect(mixed, rights, right_copies)
    _, unit_rows, unit_cols = kept_ref.shape
    for core_is in range(2):
        for x_is in range(2):
            for z_is in range(2):

                @pl.when((core == core_is) & (x == x_is) & (z == z_is))
                def _():
                    mine = total[core_is * tile : (core_is + 1) * tile]
                    other = total[(1 - core_is) * tile : (2 - core_is) * tile]
                    for xr in range(2):
                        for zr in range(2):
                            row, col = (x_is ^ xr) * unit_rows, (z_is ^ zr) * unit_cols
                            at = slice(row, row + unit_rows), slice(col, col + unit_cols)
                            kept_ref[2 * zr + xr] = mine[at]
                            sent_ref[2 * zr + xr] = other[at].astype(sent_ref.dtype)


def collect(mixed, rights, copies):
    for pair in copies:
        for copy in pair:
            copy.wait()
    terms, height, width = rights.shape
    flat = rights[...].reshape(terms * height, width)
    return jnp.dot(mixed[...], flat, preferred_element_type=jnp.float32)


def second_kernel(
    sectors,
    plan,
    square_ref,
    start_ref,
    near,
    far,
    left_own,
    left_peer,
    right_own,
    right_peer,
    kept_ref,
    sent_ref,
    start,
    vector,
    lefts,
    rights,
    mixed,
    start_sem,
    left_sems,
    right_sems,
):
    terms, tile, _ = left_own.shape
    width = 2 * tile
    half = tile // 2
    core, x, y, z = plan[0], plan[1], plan[2], plan[3]
    left_copies = place_copies((left_own, left_peer), lefts, (z, 1 - z), left_sems)
    start_copy = pltpu.make_async_copy(start_ref, start, start_sem)
    start_copy.start()
    right_copies = place_copies((right_own, right_peer), rights, (y, 1 - y), right_sems)
    for pieces, z_row in ((near, core), (far, 1 - core)):
        for xr in range(2):
            for yr in range(2):
                for sr in range(sectors):
                    row = (2 * z_row + (y ^ yr)) * tile + (x ^ xr) * half
                    at = pl.ds(pl.multiple_of(row, half), half)
                    vector[plan[4] ^ sr, at, :] = pieces[2 * xr + yr, sr]
    inner = jnp.zeros((8, width), jnp.float32)
    norm = inner
    share = vector.shape[1] // terms
    for k in range(terms):
        for copy in left_copies[k]:
            copy.wait()
        mixed[:, k * width : (k + 1) * width] = mix(plan, sectors, terms, k, lefts[k], vector)
        if k == 0:
            start_copy.wait()
        for sector in range(sectors):
            rows = slice(k * share, (k + 1) * share)
            image = vector[sector, rows, :].astype(jnp.float32)
            before = start[sector, rows, :].astype(jnp.float32)
            inner += jnp.sum((before * image).reshape(share // 8, 8, width), axis=0)
            norm += jnp.sum((image * image).reshape(share // 8, 8, width), axis=0)
    total = collect(mixed, rights, right_copies)
    extra_shape = (EXTRA_ROWS, kept_ref.shape[2])
    lane = lax.broadcasted_iota(jnp.int32, extra_shape, 1)
    zeros = jnp.zeros(extra_shape, jnp.float32)
    own_sums, z_sums = zeros, zeros
    for k, value in enumerate((square_ref[0, 0], jnp.sum(inner), jnp.sum(norm))):
        value = jnp.broadcast_to(value, extra_shape)
        own_sums = jnp.where(lane == k, value, own_sums)
        for level in range(3):
            piece = value.astype(jnp.bfloat16).astype(jnp.float32)
            z_sums = jnp.where(lane == 3 * k + level, piece, z_sums)
            value = value - piece
    for core_is in range(2):
        for x_is in range(2):
            for z_is in range(2):

                @pl.when((core == core_is) & (x == x_is) & (z == z_is))
                def _():
                    for xr in range(2):
                        for zr in range(2):
                            to = 2 * zr + xr
                            rows = slice((z_is ^ zr) * tile, ((z_is ^ zr) + 1) * tile)
                            col = (x_is ^ xr) * width
                            mine = col + core_is * tile
                            other = col + (1 - core_is) * tile
                            kept_ref[to, :tile] = total[rows, mine : mine + tile]
                            sent_ref[to, :tile] = total[rows, other : other + tile].astype(jnp.bfloat16)

    for to in range(4):
        kept_ref[to, tile:] = (own_sums, zeros, z_sums, zeros)[to]
        sent_ref[to, tile:] = zeros.astype(jnp.bfloat16)


def last_kernel(plan, own_ref, from_x, from_z, from_xz, image_ref, first_ref, out_ref):
    _, rows, cols = out_ref.shape
    first_ref[0] = image_ref[...]
    total = own_ref[:rows] + from_x[:rows].astype(jnp.float32)
    total += from_z[:rows].astype(jnp.float32) + from_xz[:rows].astype(jnp.float32)
    own_sums = own_ref[rows : rows + 8]
    z_sums = from_z[rows : rows + EXTRA_ROWS].astype(jnp.float32)[:8]
    lane = lax.broadcasted_iota(jnp.int32, own_sums.shape, 1)

    def pick(values, wanted):
        return jnp.sum(jnp.where(wanted, values, 0.0), axis=1, keepdims=True)[:1]

    sums = []
    for k in range(3):
        z_part = pick(z_sums, (lane >= 3 * k) & (lane < 3 * k + 3))
        sums.append(pick(own_sums, lane == k) + z_part)
    square, inner, norm = sums
    quotient = inner / square
    residual_square = jnp.maximum(norm - quotient * inner, 0.0)
    scale = lax.rsqrt(residual_square / square + EPSILON)
    core, x, y, z, sector = plan[0], plan[1], plan[2], plan[3], plan[4]
    sizes = plan[PLAN_BITS + 2 * sector], plan[PLAN_BITS + 2 * sector + 1]
    keep = live_block(sizes, (2 * z + y) * rows, (2 * x + core) * cols, (rows, cols))
    second = (total - quotient * image_ref[...].astype(jnp.float32)) * scale
    out_ref[0] = jnp.where(keep, second, 0.0).astype(jnp.bfloat16)


def on_device(
    wavefunction, left_environment, right_environment, sector_sizes, pairing, term_mask, coupling
):
    tile = wavefunction.shape[1]
    terms = left_environment.shape[0]
    sectors = lax.axis_size("sec") // SECTOR_BIT
    capacity = tile * GRID_ROWS
    bf16, f32 = jnp.bfloat16, jnp.float32

    def shaped(*shape, dtype=bf16):
        return jax.ShapeDtypeStruct(shape, dtype)

    index = lax.axis_index("sec").astype(jnp.int32)
    bits = [index % 2, index // XBIT % 2, index // YBIT % 2, index // ZBIT % 2, index // SECTOR_BIT]
    sizes = jnp.stack([sector_sizes[0], jnp.take(sector_sizes[1], pairing)], axis=1)
    group = index % GRID_COLS * terms

    def mine(table):
        row = lax.dynamic_slice(table, (bits[4], group), (1, terms))
        return row.reshape(terms)

    plan = jnp.concatenate([jnp.stack(bits), sizes.reshape(-1), mine(coupling), mine(term_mask)])

    tiles = []
    for y_flip in (0, YBIT):
        for sector_flip in range(0, lax.axis_size("sec"), SECTOR_BIT):
            tiles.append(exchange(wavefunction[0], y_flip | sector_flip, swapped=True))
    tiles = jnp.stack(tiles).reshape(2, sectors, tile, tile)
    gate_left, gate_right, gated = lax.optimization_barrier((left_environment, right_environment, tiles))
    tiles = jnp.stack([gated, exchange(gated, XBIT)])
    far_tiles = exchange(tiles, CORE)

    left_peer = exchange(gate_left, ZBIT)
    right_peer = exchange(gate_right, YBIT)

    def work(macs):
        return pl.CostEstimate(flops=2 * macs, bytes_accessed=terms * tile * capacity * 4, transcendentals=0)

    width = 2 * tile
    macs = terms * tile * capacity * width
    vector_shape = (sectors, capacity, width)
    unit = (4, tile // 2, width)

    def params(mib):
        return pltpu.CompilerParams(vmem_limit_bytes=mib * MIB)

    start_vector, mixed_own, square = pl.pallas_call(
        lambda *refs: start_kernel(sectors, *refs),
        out_shape=[shaped(*vector_shape), shaped(tile, terms * width), shaped(8, 128, dtype=f32)],
        in_specs=[smem(), vmem(), vmem(), anywhere()],
        out_specs=[vmem()] * 3,
        scratch_shapes=[pltpu.VMEM((terms, tile, capacity), bf16), pltpu.SemaphoreType.DMA((terms,))],
        compiler_params=params(16),
        cost_estimate=work(macs),
    )(plan, tiles, far_tiles, left_environment)
    kept, sent = pl.pallas_call(
        lambda *refs: first_kernel(sectors, *refs),
        out_shape=[shaped(*unit, dtype=f32), shaped(*unit, dtype=f32)],
        in_specs=[smem(), vmem(), vmem()] + [anywhere()] * 3,
        out_specs=[vmem()] * 2,
        scratch_shapes=[
            pltpu.VMEM((terms, tile, capacity), bf16),
            pltpu.VMEM((terms, width, capacity), bf16),
            pltpu.VMEM((width, terms * width), bf16),
            pltpu.SemaphoreType.DMA((terms,)),
            pltpu.SemaphoreType.DMA((terms, 2)),
        ],
        compiler_params=params(20),
        cost_estimate=work(3 * macs),
    )(plan, start_vector, mixed_own, left_peer, right_environment, right_peer)

    def live(row_start, col_start, shape):
        mine = jnp.take(sizes, bits[4], axis=0)
        return live_block((mine[0], mine[1]), row_start, col_start, shape)

    summed = kept + exchange(sent, CORE)
    image_unit = (
        summed[0]
        + exchange(summed[1].astype(bf16), XBIT).astype(f32)
        + exchange(summed[2].astype(bf16), ZBIT).astype(f32)
        + exchange(summed[3].astype(bf16), XBIT | ZBIT).astype(f32)
    )
    rows, cols = unit[1:]
    keep = live((2 * bits[0] + bits[2]) * tile + bits[1] * rows, bits[3] * cols, (rows, cols))
    units = jnp.where(keep, image_unit, 0.0).astype(bf16)[None]
    flip = SECTOR_BIT
    while flip < lax.axis_size("sec"):
        units = jnp.concatenate([units, exchange(units, flip)])
        flip *= 2
    units = jnp.stack(
        [units, exchange(units, YBIT), exchange(units, XBIT), exchange(units, XBIT | YBIT)]
    )
    far_units = exchange(units, CORE)
    mine = jnp.where(bits[0] == bits[1], units[:, 0], far_units[:, 0])
    mine = jnp.where(bits[1] == 0, jnp.concatenate([mine[0], mine[2]]), jnp.concatenate([mine[2], mine[0]]))
    image_tile = jnp.where(bits[0] == 0, mine[:, :tile], mine[:, tile:])
    first_tile = exchange(image_tile, 0, swapped=True)
    part = (4, tile + EXTRA_ROWS, tile)
    kept, sent = pl.pallas_call(
        lambda *refs: second_kernel(sectors, *refs),
        out_shape=[shaped(*part, dtype=f32), shaped(*part)],
        in_specs=[smem(), vmem(), anywhere(), vmem(), vmem()] + [anywhere()] * 4,
        out_specs=[vmem()] * 2,
        scratch_shapes=[
            pltpu.VMEM(vector_shape, bf16),
            pltpu.VMEM(vector_shape, bf16),
            pltpu.VMEM((terms, width, capacity), bf16),
            pltpu.VMEM((terms, width, capacity), bf16),
            pltpu.VMEM((width, terms * width), bf16),
            pltpu.SemaphoreType.DMA,
            pltpu.SemaphoreType.DMA((terms, 2)),
            pltpu.SemaphoreType.DMA((terms, 2)),
        ],
        compiler_params=params(28),
        cost_estimate=work(4 * macs),
    )(
        plan,
        square,
        start_vector,
        units,
        far_units,
        left_environment,
        left_peer,
        right_environment,
        right_peer,
    )
    summed = kept + exchange(sent, CORE).astype(f32)
    first, second = pl.pallas_call(
        last_kernel,
        out_shape=[shaped(1, tile, tile)] * 2,
        in_specs=[smem()] + [vmem()] * 5,
        out_specs=[vmem()] * 2,
        compiler_params=pltpu.CompilerParams(vmem_limit_bytes=4 * MIB),
    )(
        plan,
        summed[0],
        exchange(summed[1].astype(bf16), XBIT),
        exchange(summed[2].astype(bf16), ZBIT),
        exchange(summed[3].astype(bf16), XBIT | ZBIT),
        first_tile,
    )
    return first, second


def solution(mesh):
    return jax.shard_map(
        on_device,
        mesh=mesh,
        in_specs=(
            P(("groups", "sec"), None, None),
            P(("groups", "sec"), None, None),
            P(("groups", "sec"), None, None),
            P(None, "groups"),
            P("groups"),
            P("groups", None),
            P("groups", None),
        ),
        out_specs=(P(("groups", "sec"), None, None), P(("groups", "sec"), None, None)),
        check_vma=False,
    )
```

```python
import jax
import jax.numpy as jnp
from jax import lax
from jax.experimental import pallas as pl
from jax.experimental.pallas import tpu as pltpu
from jax.sharding import PartitionSpec as P

GRID_ROWS = 4
GRID_COLS = 4
CORE, XBIT, YBIT, ZBIT = 1, 2, 4, 8
SECTOR_BIT = GRID_ROWS * GRID_COLS
EPSILON = 1e-06
EXTRA_ROWS = 16
MIB = 2**20
START_COST = 8
PLAN_BITS = 5


def exchange(block, flip, swapped=False):
    route = []
    for i in range(lax.axis_size("sec")):
        x, z = i // XBIT % 2, i // ZBIT % 2
        moved = i - x * XBIT - z * ZBIT + z * XBIT + x * ZBIT if swapped else i
        route.append((i, moved ^ flip))
    return lax.ppermute(block, "sec", route)


def smem():
    return pl.BlockSpec(memory_space=pltpu.SMEM)


def vmem():
    return pl.BlockSpec(memory_space=pltpu.VMEM)


def anywhere():
    return pl.BlockSpec(memory_space=pl.ANY)


def live_block(sizes, row_start, col_start, shape):
    rows = row_start + lax.broadcasted_iota(jnp.int32, shape, 0)
    cols = col_start + lax.broadcasted_iota(jnp.int32, shape, 1)
    return (rows < sizes[0]) & (cols < sizes[1])


def place_copies(sources, target, places, sems):
    tile = sources[0].shape[1]
    found = []
    for k in range(sources[0].shape[0]):
        pair = []
        for slot in range(2):
            row = pl.multiple_of(places[slot] * tile, tile)
            copy = pltpu.make_async_copy(
                sources[slot].at[k], target.at[k, pl.ds(row, tile)], sems.at[k, slot]
            )
            copy.start()
            pair.append(copy)
        found.append(pair)
    return found


def term_of(plan, sectors, terms, k):
    base = PLAN_BITS + 2 * sectors
    return plan[base + k], plan[base + terms + k].astype(jnp.float32)


def mix(plan, sectors, terms, k, left, vector):
    source, weight = term_of(plan, sectors, terms, k)
    product = jnp.dot(left, vector[source], preferred_element_type=jnp.float32)
    return (product * weight).astype(jnp.bfloat16)


def start_kernel(
    sectors, plan, near, far, left_own, right_own, vector, mixed_ref, square_ref, lefts, rights, sems
):
    terms, tile, _ = left_own.shape
    width = 2 * tile
    core, x, y, z = plan[0], plan[1], plan[2], plan[3]
    copies = []
    for k in range(terms):
        copy = pltpu.make_async_copy(left_own.at[k], lefts.at[k], sems.at[k])
        copy.start()
        copies.append(copy)
    copy = pltpu.make_async_copy(right_own, rights, sems.at[terms])
    copy.start()
    copies.append(copy)
    square = jnp.zeros((8, width), jnp.float32)
    for xr in range(2):
        for yr in range(2):
            for sr in range(sectors):
                sector = plan[4] ^ sr
                row = (2 * (x ^ xr) + (y ^ yr)) * tile
                sizes = plan[PLAN_BITS + 2 * sector], plan[PLAN_BITS + 2 * sector + 1]
                mine, other = near[xr, yr, sr], far[xr, yr, sr]
                low = jnp.where(core == 0, mine, other).astype(jnp.float32)
                high = jnp.where(core == 0, other, mine).astype(jnp.float32)
                both = jnp.concatenate([low, high], axis=1)
                both = jnp.where(live_block(sizes, row, z * width, both.shape), both, 0.0)
                square += jnp.sum((both * both).reshape(tile // 8, 8, width), axis=0)
                at = pl.ds(pl.multiple_of(row, tile), tile)
                vector[sector, at, :] = both.astype(jnp.bfloat16)
    square_ref[...] = jnp.broadcast_to(jnp.sum(square), square_ref.shape)
    for k in range(terms):
        copies[k].wait()
        mixed_ref[:, k * width : (k + 1) * width] = mix(plan, sectors, terms, k, lefts[k], vector)
    copies[terms].wait()


def first_kernel(
    sectors,
    plan,
    vector,
    mixed_own,
    left_own,
    left_peer,
    right_own,
    right_peer,
    kept_ref,
    sent_ref,
    lefts,
    rights,
    mixed,
    left_sems,
    right_sems,
    own_sem,
):
    terms, tile, _ = left_peer.shape
    width = 2 * tile
    core, x, y, z = plan[0], plan[1], plan[2], plan[3]
    peer = pl.ds(pl.multiple_of((1 - z) * tile, tile), tile)
    left_copies = []
    for k in range(terms):
        copy = pltpu.make_async_copy(left_peer.at[k], lefts.at[k, peer], left_sems.at[k])
        copy.start()
        left_copies.append(copy)
    right_copies = place_copies((right_own, right_peer), rights, (y, 1 - y), right_sems)
    own = pl.ds(pl.multiple_of(z * tile, tile), tile)
    left_copy = pltpu.make_async_copy(left_own, lefts.at[:, own], own_sem)
    left_copy.start()
    mixed[own, :] = mixed_own[...]
    for k in range(terms):
        left_copies[k].wait()
        mixed[peer, k * width : (k + 1) * width] = mix(plan, sectors, terms, k, lefts[k, peer], vector)
    total = collect(mixed, rights, right_copies)
    left_copy.wait()
    sizes = plan[PLAN_BITS + 2 * plan[4]], plan[PLAN_BITS + 2 * plan[4] + 1]
    parts = []
    for z_row in range(2):
        part = total[z_row * tile : (z_row + 1) * tile]
        keep = live_block(sizes, (2 * z_row + y) * tile, 0, part.shape)
        parts.append(jnp.where(keep, part, 0.0))
    _, unit_rows, unit_cols = kept_ref.shape
    for core_is in range(2):
        for x_is in range(2):
            for z_is in range(2):

                @pl.when((core == core_is) & (x == x_is) & (z == z_is))
                def _():
                    mine, other = parts[core_is], parts[1 - core_is]
                    for xr in range(2):
                        for zr in range(2):
                            row, col = (x_is ^ xr) * unit_rows, (z_is ^ zr) * unit_cols
                            at = slice(row, row + unit_rows), slice(col, col + unit_cols)
                            kept_ref[2 * zr + xr] = mine[at]
                            sent_ref[2 * zr + xr] = other[at].astype(sent_ref.dtype)


def collect(mixed, rights, copies):
    for pair in copies:
        for copy in pair:
            copy.wait()
    terms, height, width = rights.shape
    flat = rights[...].reshape(terms * height, width)
    return jnp.dot(mixed[...], flat, preferred_element_type=jnp.float32)


def second_kernel(
    sectors,
    plan,
    square_ref,
    start,
    near,
    far,
    lefts,
    rights,
    kept_ref,
    sent_ref,
    tiles_ref,
    vector,
    mixed,
):
    terms, width, _ = lefts.shape
    tile = width // 2
    half = tile // 2
    core, x, y, z = plan[0], plan[1], plan[2], plan[3]
    for pieces, z_row in ((near, core), (far, 1 - core)):
        for xr in range(2):
            for yr in range(2):
                for sr in range(sectors):
                    row = (2 * z_row + (y ^ yr)) * tile + (x ^ xr) * half
                    at = pl.ds(pl.multiple_of(row, half), half)
                    vector[plan[4] ^ sr, at, :] = pieces[2 * xr + yr, sr]
    inner = jnp.zeros((8, width), jnp.float32)
    norm = inner
    for k in range(terms):
        mixed[:, k * width : (k + 1) * width] = mix(plan, sectors, terms, k, lefts[k], vector)
        if k < 4:
            for sr in range(sectors):
                row = (2 * core + (y ^ (k % 2))) * tile + (x ^ (k // 2)) * half
                at = pl.ds(pl.multiple_of(row, half), half)
                image = near[k, sr].astype(jnp.float32)
                before = start[plan[4] ^ sr, at, :].astype(jnp.float32)
                inner += jnp.sum((before * image).reshape(half // 8, 8, width), axis=0)
                norm += jnp.sum((image * image).reshape(half // 8, 8, width), axis=0)
    total = collect(mixed, rights, [])
    extra_shape = (EXTRA_ROWS, kept_ref.shape[2])
    lane = lax.broadcasted_iota(jnp.int32, extra_shape, 1)
    zeros = jnp.zeros(extra_shape, jnp.float32)
    own_sums, z_sums = zeros, zeros
    for k, value in enumerate((0.5 * square_ref[0, 0], jnp.sum(inner), jnp.sum(norm))):
        value = jnp.broadcast_to(value, extra_shape)
        own_sums = jnp.where(lane == k, value, own_sums)
        for level in range(3):
            piece = value.astype(jnp.bfloat16).astype(jnp.float32)
            z_sums = jnp.where(lane == 9 * core + 3 * k + level, piece, z_sums)
            value = value - piece

    def packed(block, row, col):
        halves = [block[row + r : row + r + half, col : col + tile] for r in (0, half)]
        return jnp.concatenate(halves, axis=1)

    image_tiles = []
    for z_row in (z, 1 - z):
        row = pl.multiple_of((2 * z_row + y) * tile, tile)
        image_tiles.append(vector[plan[4], pl.ds(row, tile), :].astype(jnp.float32))
    for core_is in range(2):

        @pl.when(core == core_is)
        def _():
            for k in range(2):
                tiles_ref[k] = packed(image_tiles[k], 0, core_is * tile).astype(tiles_ref.dtype)

        for x_is in range(2):
            for z_is in range(2):

                @pl.when((core == core_is) & (x == x_is) & (z == z_is))
                def _():
                    for xr in range(2):
                        for zr in range(2):
                            row = (z_is ^ zr) * tile
                            col = (x_is ^ xr) * width
                            mine = packed(total, row, col + core_is * tile)
                            other = packed(total, row, col + (1 - core_is) * tile)
                            kept_ref[2 * zr + xr, :half] = mine
                            sent_ref[2 * zr + xr, :half] = other

    for to in range(4):
        kept_ref[to, half:] = (own_sums, zeros, z_sums, zeros)[to]
        sent_ref[to, half:] = (own_sums, zeros, z_sums, zeros)[to]


def last_kernel(plan, own_ref, from_x, from_z, from_xz, tiles_ref, first_ref, out_ref):
    _, rows, cols = out_ref.shape
    half = rows // 2
    core, x, y, z, sector = plan[0], plan[1], plan[2], plan[3], plan[4]
    total = own_ref[:half] + from_x[:half].astype(jnp.float32)
    total += from_z[:half].astype(jnp.float32) + from_xz[:half].astype(jnp.float32)
    own_sums = own_ref[half : half + 8]
    z_sums = from_z[half : half + EXTRA_ROWS].astype(jnp.float32)[:8]
    sent_tile = from_z[half + EXTRA_ROWS :].astype(jnp.float32)
    image = jnp.where(x == z, tiles_ref[0].astype(jnp.float32), sent_tile)
    lane = lax.broadcasted_iota(jnp.int32, own_sums.shape, 1)

    def pick(values, wanted):
        return jnp.sum(jnp.where(wanted, values, 0.0), axis=1, keepdims=True)[:1]

    sums = []
    for k in range(3):
        z_part = pick(z_sums, (lane % 9 // 3 == k) & (lane < 18))
        sums.append(pick(own_sums, lane == k) + z_part)
    square, inner, norm = sums
    quotient = inner / square
    residual_square = jnp.maximum(norm - quotient * inner, 0.0)
    scale = lax.rsqrt(residual_square / square + EPSILON)
    sizes = plan[PLAN_BITS + 2 * sector], plan[PLAN_BITS + 2 * sector + 1]
    second = (total - quotient * image) * scale
    for k in range(2):
        at = slice(k * half, (k + 1) * half)
        part = slice(k * cols, (k + 1) * cols)
        first_ref[0, at] = image[:, part].astype(jnp.bfloat16)
        row = (2 * z + y) * rows + k * half
        keep = live_block(sizes, row, (2 * x + core) * cols, (half, cols))
        out_ref[0, at] = jnp.where(keep, second[:, part], 0.0).astype(jnp.bfloat16)


def on_device(
    wavefunction, left_environment, right_environment, sector_sizes, pairing, term_mask, coupling
):
    tile = wavefunction.shape[1]
    terms = left_environment.shape[0]
    sectors = lax.axis_size("sec") // SECTOR_BIT
    capacity = tile * GRID_ROWS
    bf16, f32 = jnp.bfloat16, jnp.float32

    def shaped(*shape, dtype=bf16):
        return jax.ShapeDtypeStruct(shape, dtype)

    index = lax.axis_index("sec").astype(jnp.int32)
    bits = [index % 2, index // XBIT % 2, index // YBIT % 2, index // ZBIT % 2, index // SECTOR_BIT]
    sizes = jnp.stack([sector_sizes[0], jnp.take(sector_sizes[1], pairing)], axis=1)
    group = index % GRID_COLS * terms

    def mine(table):
        row = lax.dynamic_slice(table, (bits[4], group), (1, terms))
        return row.reshape(terms)

    plan = jnp.concatenate([jnp.stack(bits), sizes.reshape(-1), mine(coupling), mine(term_mask)])

    tiles = []
    for y_flip in (0, YBIT):
        for sector_flip in range(0, lax.axis_size("sec"), SECTOR_BIT):
            tiles.append(exchange(wavefunction[0], y_flip | sector_flip, swapped=True))
    tiles = jnp.stack(tiles).reshape(2, sectors, tile, tile)
    tiles = jnp.stack([tiles, exchange(tiles, XBIT)])
    far_tiles = exchange(tiles, CORE)

    left_peer = exchange(left_environment, ZBIT)
    right_peer = exchange(right_environment, YBIT)

    def work(macs):
        return pl.CostEstimate(flops=2 * macs, bytes_accessed=terms * tile * capacity * 4, transcendentals=0)

    width = 2 * tile
    macs = terms * tile * capacity * width
    vector_shape = (sectors, capacity, width)
    unit = (4, tile // 2, width)

    def params(mib):
        return pltpu.CompilerParams(vmem_limit_bytes=mib * MIB)

    environments = shaped(terms, width, capacity)
    start_vector, mixed_own, square, left_own, right_own = pl.pallas_call(
        lambda *refs: start_kernel(sectors, *refs),
        out_shape=[shaped(*vector_shape), shaped(tile, terms * width), shaped(8, 128, dtype=f32)]
        + [shaped(terms, tile, capacity)] * 2,
        in_specs=[smem(), vmem(), vmem(), anywhere(), anywhere()],
        out_specs=[vmem()] * 5,
        scratch_shapes=[pltpu.SemaphoreType.DMA((terms + 1,))],
        compiler_params=params(16),
        cost_estimate=work(START_COST * macs),
    )(plan, tiles, far_tiles, left_environment, right_environment)
    kept, sent, lefts, rights = pl.pallas_call(
        lambda *refs: first_kernel(sectors, *refs),
        out_shape=[shaped(*unit, dtype=f32), shaped(*unit, dtype=f32), environments, environments],
        in_specs=[smem(), vmem(), vmem()] + [anywhere()] * 4,
        out_specs=[vmem()] * 4,
        scratch_shapes=[
            pltpu.VMEM((width, terms * width), bf16),
            pltpu.SemaphoreType.DMA((terms,)),
            pltpu.SemaphoreType.DMA((terms, 2)),
            pltpu.SemaphoreType.DMA,
        ],
        compiler_params=params(20),
        cost_estimate=work(3 * macs),
    )(plan, start_vector, mixed_own, left_own, left_peer, right_own, right_peer)

    summed = kept + exchange(sent, CORE)
    image_unit = (
        summed[0]
        + exchange(summed[1].astype(bf16), XBIT).astype(f32)
        + exchange(summed[2].astype(bf16), ZBIT).astype(f32)
        + exchange(summed[3].astype(bf16), XBIT | ZBIT).astype(f32)
    )
    units = image_unit.astype(bf16)[None]
    flip = SECTOR_BIT
    while flip < lax.axis_size("sec"):
        units = jnp.concatenate([units, exchange(units, flip)])
        flip *= 2
    units = jnp.stack(
        [units, exchange(units, YBIT), exchange(units, XBIT), exchange(units, XBIT | YBIT)]
    )
    far_units = exchange(units, CORE)
    half = tile // 2
    part = (4, half + EXTRA_ROWS, width)
    kept, sent, image_tiles = pl.pallas_call(
        lambda *refs: second_kernel(sectors, *refs),
        out_shape=[shaped(*part, dtype=f32)] * 2 + [shaped(2, half, width)],
        in_specs=[smem()] + [vmem()] * 6,
        out_specs=[vmem()] * 3,
        scratch_shapes=[pltpu.VMEM(vector_shape, bf16), pltpu.VMEM((width, terms * width), bf16)],
        compiler_params=params(24),
        cost_estimate=work(4 * macs),
    )(
        plan,
        square,
        start_vector,
        units,
        far_units,
        lefts,
        rights,
    )
    summed = kept + exchange(sent, CORE)
    to_z = jnp.concatenate([summed[2].astype(bf16), image_tiles[1]])
    first, second = pl.pallas_call(
        last_kernel,
        out_shape=[shaped(1, tile, tile)] * 2,
        in_specs=[smem()] + [vmem()] * 5,
        out_specs=[vmem()] * 2,
        compiler_params=params(4),
    )(
        plan,
        summed[0],
        exchange(summed[1].astype(bf16), XBIT),
        exchange(to_z, ZBIT),
        exchange(summed[3].astype(bf16), XBIT | ZBIT),
        image_tiles,
    )
    return first, second


def solution(mesh):
    return jax.shard_map(
        on_device,
        mesh=mesh,
        in_specs=(
            P(("groups", "sec"), None, None),
            P(("groups", "sec"), None, None),
            P(("groups", "sec"), None, None),
            P(None, "groups"),
            P("groups"),
            P("groups", None),
            P("groups", None),
        ),
        out_specs=(P(("groups", "sec"), None, None), P(("groups", "sec"), None, None)),
        check_vma=False,
    )
```

```python
import jax
import jax.numpy as jnp
from jax import lax
from jax.experimental import pallas as pl
from jax.experimental.pallas import tpu as pltpu
from jax.sharding import PartitionSpec as P

GRID_ROWS = 4
GRID_COLS = 4
CORE, XBIT, YBIT, ZBIT = 1, 2, 4, 8
SECTOR_BIT = GRID_ROWS * GRID_COLS
EPSILON = 1e-06
EXTRA_ROWS = 16
MIB = 2**20
START_COST = 8
PLAN_BITS = 5


def exchange(block, flip):
    return lax.ppermute(block, "sec", [(i, i ^ flip) for i in range(lax.axis_size("sec"))])


def spread(tile, flip):
    route = []
    for i in range(lax.axis_size("sec")):
        x, z = i // XBIT % 2, i // ZBIT % 2
        new_x = x ^ z if flip >= SECTOR_BIT else z
        route.append((i, i + (new_x - x) * XBIT + (x - z) * ZBIT ^ flip))
    return lax.ppermute(tile, "sec", route)


def smem():
    return pl.BlockSpec(memory_space=pltpu.SMEM)


def vmem():
    return pl.BlockSpec(memory_space=pltpu.VMEM)


def anywhere():
    return pl.BlockSpec(memory_space=pl.ANY)


def live_block(sizes, row_start, col_start, shape):
    rows = row_start + lax.broadcasted_iota(jnp.int32, shape, 0)
    cols = col_start + lax.broadcasted_iota(jnp.int32, shape, 1)
    return (rows < sizes[0]) & (cols < sizes[1])


def place_copies(sources, target, places, sems):
    tile = sources[0].shape[1]
    found = []
    for k in range(sources[0].shape[0]):
        pair = []
        for slot in range(2):
            row = pl.multiple_of(places[slot] * tile, tile)
            copy = pltpu.make_async_copy(
                sources[slot].at[k], target.at[k, pl.ds(row, tile)], sems.at[k, slot]
            )
            copy.start()
            pair.append(copy)
        found.append(pair)
    return found


def term_of(plan, sectors, terms, k):
    base = PLAN_BITS + 2 * sectors
    return plan[base + k], plan[base + terms + k].astype(jnp.float32)


def mix(plan, sectors, terms, k, left, vector):
    source, weight = term_of(plan, sectors, terms, k)
    product = jnp.dot(left, vector[source], preferred_element_type=jnp.float32)
    return (product * weight).astype(jnp.bfloat16)


def start_kernel(
    sectors, plan, near, far, left_own, right_own, vector, mixed_ref, square_ref, lefts, rights, sems
):
    terms, tile, _ = left_own.shape
    width = 2 * tile
    core, x, y, z = plan[0], plan[1], plan[2], plan[3]
    copies = []
    for k in range(terms):
        copy = pltpu.make_async_copy(left_own.at[k], lefts.at[k], sems.at[k])
        copy.start()
        copies.append(copy)
    copy = pltpu.make_async_copy(right_own, rights, sems.at[terms])
    copy.start()
    copies.append(copy)
    square = jnp.zeros((8, width), jnp.float32)
    for xr in range(2):
        for yr in range(2):
            for sr in range(sectors):
                sector = plan[4] ^ sr
                z_row = x ^ xr ^ z if sr else x ^ xr
                row = (2 * z_row + (y ^ yr)) * tile
                sizes = plan[PLAN_BITS + 2 * sector], plan[PLAN_BITS + 2 * sector + 1]
                mine, other = near[xr, yr, sr], far[xr, yr, sr]
                low = jnp.where(core == 0, mine, other).astype(jnp.float32)
                high = jnp.where(core == 0, other, mine).astype(jnp.float32)
                top = jnp.concatenate([low[:, :tile], high[:, :tile]], axis=1)
                bottom = jnp.concatenate([low[:, tile:], high[:, tile:]], axis=1)
                both = jnp.concatenate([top, bottom], axis=0)
                both = jnp.where(live_block(sizes, row, z * width, both.shape), both, 0.0)
                square += jnp.sum((both * both).reshape(tile // 8, 8, width), axis=0)
                at = pl.ds(pl.multiple_of(row, tile), tile)
                vector[sector, at, :] = both.astype(jnp.bfloat16)
    square_ref[...] = jnp.broadcast_to(jnp.sum(square), square_ref.shape)
    for k in range(terms):
        copies[k].wait()
        mixed_ref[:, k * width : (k + 1) * width] = mix(plan, sectors, terms, k, lefts[k], vector)
    copies[terms].wait()


def first_kernel(
    sectors,
    plan,
    vector,
    mixed_own,
    left_own,
    left_peer,
    right_own,
    right_peer,
    kept_ref,
    sent_ref,
    lefts,
    rights,
    mixed,
    left_sems,
    right_sems,
):
    terms, tile, _ = left_peer.shape
    width = 2 * tile
    core, x, y, z = plan[0], plan[1], plan[2], plan[3]
    peer = pl.ds(pl.multiple_of((1 - z) * tile, tile), tile)
    right_copies = place_copies((right_own, right_peer), rights, (y, 1 - y), right_sems)
    own = pl.ds(pl.multiple_of(z * tile, tile), tile)
    left_copies = [
        pltpu.make_async_copy(left_own, lefts.at[:, own], left_sems.at[0]),
        pltpu.make_async_copy(left_peer, lefts.at[:, peer], left_sems.at[1]),
    ]
    for copy in left_copies:
        copy.start()
    mixed[own, :] = mixed_own[...]
    for k in range(terms):
        mixed[peer, k * width : (k + 1) * width] = mix(plan, sectors, terms, k, left_peer[k], vector)
    total = collect(mixed, rights, right_copies)
    for copy in left_copies:
        copy.wait()
    sizes = plan[PLAN_BITS + 2 * plan[4]], plan[PLAN_BITS + 2 * plan[4] + 1]
    parts = []
    for z_row in range(2):
        part = total[z_row * tile : (z_row + 1) * tile]
        keep = live_block(sizes, (2 * z_row + y) * tile, 0, part.shape)
        parts.append(jnp.where(keep, part, 0.0))
    _, unit_rows, unit_cols = kept_ref.shape
    for core_is in range(2):
        for x_is in range(2):
            for z_is in range(2):

                @pl.when((core == core_is) & (x == x_is) & (z == z_is))
                def _():
                    mine, other = parts[core_is], parts[1 - core_is]
                    for xr in range(2):
                        for zr in range(2):
                            row, col = (x_is ^ xr) * unit_rows, (z_is ^ zr) * unit_cols
                            at = slice(row, row + unit_rows), slice(col, col + unit_cols)
                            kept_ref[2 * zr + xr] = mine[at]
                            sent_ref[2 * zr + xr] = other[at].astype(sent_ref.dtype)


def collect(mixed, rights, copies):
    for pair in copies:
        for copy in pair:
            copy.wait()
    terms, height, width = rights.shape
    flat = rights[...].reshape(terms * height, width)
    return jnp.dot(mixed[...], flat, preferred_element_type=jnp.float32)


def second_kernel(
    sectors,
    plan,
    square_ref,
    start,
    near,
    far,
    lefts,
    rights,
    kept_ref,
    sent_ref,
    tiles_ref,
    vector,
    mixed,
):
    terms, width, _ = lefts.shape
    tile = width // 2
    half = tile // 2
    core, x, y, z = plan[0], plan[1], plan[2], plan[3]
    for pieces, z_row in ((near, core), (far, 1 - core)):
        for xr in range(2):
            for yr in range(2):
                for sr in range(sectors):
                    row = (2 * z_row + (y ^ yr)) * tile + (x ^ xr) * half
                    at = pl.ds(pl.multiple_of(row, half), half)
                    vector[plan[4] ^ sr, at, :] = pieces[2 * xr + yr, sr]
    inner = jnp.zeros((8, width), jnp.float32)
    norm = inner
    for k in range(terms):
        mixed[:, k * width : (k + 1) * width] = mix(plan, sectors, terms, k, lefts[k], vector)
        if k < 4:
            for sr in range(sectors):
                row = (2 * core + (y ^ (k % 2))) * tile + (x ^ (k // 2)) * half
                at = pl.ds(pl.multiple_of(row, half), half)
                image = near[k, sr].astype(jnp.float32)
                before = start[plan[4] ^ sr, at, :].astype(jnp.float32)
                inner += jnp.sum((before * image).reshape(half // 8, 8, width), axis=0)
                norm += jnp.sum((image * image).reshape(half // 8, 8, width), axis=0)
    total = collect(mixed, rights, [])
    extra_shape = (EXTRA_ROWS, kept_ref.shape[2])
    lane = lax.broadcasted_iota(jnp.int32, extra_shape, 1)
    zeros = jnp.zeros(extra_shape, jnp.float32)
    own_sums, z_sums = zeros, zeros
    for k, value in enumerate((0.5 * square_ref[0, 0], jnp.sum(inner), jnp.sum(norm))):
        value = jnp.broadcast_to(value, extra_shape)
        own_sums = jnp.where(lane == k, value, own_sums)
        for level in range(3):
            piece = value.astype(jnp.bfloat16).astype(jnp.float32)
            z_sums = jnp.where(lane == 9 * core + 3 * k + level, piece, z_sums)
            value = value - piece

    def packed(block, row, col):
        halves = [block[row + r : row + r + half, col : col + tile] for r in (0, half)]
        return jnp.concatenate(halves, axis=1)

    image_tiles = []
    for z_row in (z, 1 - z):
        row = pl.multiple_of((2 * z_row + y) * tile, tile)
        image_tiles.append(vector[plan[4], pl.ds(row, tile), :].astype(jnp.float32))
    for core_is in range(2):

        @pl.when(core == core_is)
        def _():
            for k in range(2):
                tiles_ref[k] = packed(image_tiles[k], 0, core_is * tile).astype(tiles_ref.dtype)

        for x_is in range(2):
            for z_is in range(2):

                @pl.when((core == core_is) & (x == x_is) & (z == z_is))
                def _():
                    for xr in range(2):
                        for zr in range(2):
                            row = (z_is ^ zr) * tile
                            col = (x_is ^ xr) * width
                            mine = packed(total, row, col + core_is * tile)
                            other = packed(total, row, col + (1 - core_is) * tile)
                            kept_ref[2 * zr + xr, :half] = mine
                            sent_ref[2 * zr + xr, :half] = other

    for to in range(4):
        kept_ref[to, half:] = (own_sums, zeros, z_sums, zeros)[to]
        sent_ref[to, half:] = (own_sums, zeros, z_sums, zeros)[to]


def last_kernel(plan, own_ref, from_x, from_z, from_xz, tiles_ref, got_ref, first_ref, out_ref):
    _, rows, cols = out_ref.shape
    half = rows // 2
    core, x, y, z, sector = plan[0], plan[1], plan[2], plan[3], plan[4]
    total = own_ref[:half] + from_x[:half].astype(jnp.float32)
    total += from_z[:half].astype(jnp.float32) + from_xz[:half].astype(jnp.float32)
    own_sums = own_ref[half : half + 8]
    z_sums = from_z[half : half + EXTRA_ROWS].astype(jnp.float32)[:8]
    image = jnp.where(x == z, tiles_ref[0], got_ref[...]).astype(jnp.float32)
    lane = lax.broadcasted_iota(jnp.int32, own_sums.shape, 1)

    def pick(values, wanted):
        return jnp.sum(jnp.where(wanted, values, 0.0), axis=1, keepdims=True)[:1]

    sums = []
    for k in range(3):
        z_part = pick(z_sums, (lane % 9 // 3 == k) & (lane < 18))
        sums.append(pick(own_sums, lane == k) + z_part)
    square, inner, norm = sums
    quotient = inner / square
    residual_square = jnp.maximum(norm - quotient * inner, 0.0)
    scale = lax.rsqrt(residual_square / square + EPSILON)
    sizes = plan[PLAN_BITS + 2 * sector], plan[PLAN_BITS + 2 * sector + 1]
    second = (total - quotient * image) * scale
    for k in range(2):
        at = slice(k * half, (k + 1) * half)
        part = slice(k * cols, (k + 1) * cols)
        first_ref[0, at] = image[:, part].astype(jnp.bfloat16)
        row = (2 * z + y) * rows + k * half
        keep = live_block(sizes, row, (2 * x + core) * cols, (half, cols))
        out_ref[0, at] = jnp.where(keep, second[:, part], 0.0).astype(jnp.bfloat16)


def on_device(
    wavefunction, left_environment, right_environment, sector_sizes, pairing, term_mask, coupling
):
    tile = wavefunction.shape[1]
    terms = left_environment.shape[0]
    sectors = lax.axis_size("sec") // SECTOR_BIT
    capacity = tile * GRID_ROWS
    bf16, f32 = jnp.bfloat16, jnp.float32

    def shaped(*shape, dtype=bf16):
        return jax.ShapeDtypeStruct(shape, dtype)

    index = lax.axis_index("sec").astype(jnp.int32)
    bits = [index % 2, index // XBIT % 2, index // YBIT % 2, index // ZBIT % 2, index // SECTOR_BIT]
    sizes = jnp.stack([sector_sizes[0], jnp.take(sector_sizes[1], pairing)], axis=1)
    group = index % GRID_COLS * terms

    def mine(table):
        row = lax.dynamic_slice(table, (bits[4], group), (1, terms))
        return row.reshape(terms)

    plan = jnp.concatenate([jnp.stack(bits), sizes.reshape(-1), mine(coupling), mine(term_mask)])

    start_tile = jnp.concatenate([wavefunction[0, : tile // 2], wavefunction[0, tile // 2 :]], axis=1)
    tiles = []
    for y_flip in (0, YBIT):
        for sector_flip in range(0, lax.axis_size("sec"), SECTOR_BIT):
            tiles.append(spread(start_tile, y_flip | sector_flip))
    tiles = jnp.stack(tiles).reshape(2, sectors, tile // 2, 2 * tile)
    tiles = jnp.stack([tiles, exchange(tiles, XBIT)])
    far_tiles = exchange(tiles, CORE)

    left_peer = exchange(left_environment, ZBIT)
    right_peer = exchange(right_environment, YBIT)

    def work(macs):
        return pl.CostEstimate(flops=2 * macs, bytes_accessed=terms * tile * capacity * 4, transcendentals=0)

    width = 2 * tile
    macs = terms * tile * capacity * width
    vector_shape = (sectors, capacity, width)
    unit = (4, tile // 2, width)

    def params(mib):
        return pltpu.CompilerParams(vmem_limit_bytes=mib * MIB)

    environments = shaped(terms, width, capacity)
    start_vector, mixed_own, square, left_own, right_own = pl.pallas_call(
        lambda *refs: start_kernel(sectors, *refs),
        out_shape=[shaped(*vector_shape), shaped(tile, terms * width), shaped(8, 128, dtype=f32)]
        + [shaped(terms, tile, capacity)] * 2,
        in_specs=[smem(), vmem(), vmem(), anywhere(), anywhere()],
        out_specs=[vmem()] * 5,
        scratch_shapes=[pltpu.SemaphoreType.DMA((terms + 1,))],
        compiler_params=params(16),
        cost_estimate=work(START_COST * macs),
    )(plan, tiles, far_tiles, left_environment, right_environment)
    kept, sent, lefts, rights = pl.pallas_call(
        lambda *refs: first_kernel(sectors, *refs),
        out_shape=[shaped(*unit, dtype=f32), shaped(*unit, dtype=f32), environments, environments],
        in_specs=[smem()] + [vmem()] * 6,
        out_specs=[vmem()] * 4,
        scratch_shapes=[
            pltpu.VMEM((width, terms * width), bf16),
            pltpu.SemaphoreType.DMA((2,)),
            pltpu.SemaphoreType.DMA((terms, 2)),
        ],
        compiler_params=params(20),
        cost_estimate=work(3 * macs),
    )(plan, start_vector, mixed_own, left_own, left_peer, right_own, right_peer)

    summed = kept + exchange(sent, CORE)
    image_unit = (
        summed[0]
        + exchange(summed[1].astype(bf16), XBIT).astype(f32)
        + exchange(summed[2].astype(bf16), ZBIT).astype(f32)
        + exchange(summed[3].astype(bf16), XBIT | ZBIT).astype(f32)
    )
    units = image_unit.astype(bf16)[None]
    flip = SECTOR_BIT
    while flip < lax.axis_size("sec"):
        units = jnp.concatenate([units, exchange(units, flip)])
        flip *= 2
    units = jnp.stack(
        [units, exchange(units, YBIT), exchange(units, XBIT), exchange(units, XBIT | YBIT)]
    )
    far_units = exchange(units, CORE)
    half = tile // 2
    part = (4, half + EXTRA_ROWS, width)
    kept, sent, image_tiles = pl.pallas_call(
        lambda *refs: second_kernel(sectors, *refs),
        out_shape=[shaped(*part, dtype=f32)] * 2 + [shaped(2, half, width)],
        in_specs=[smem()] + [vmem()] * 6,
        out_specs=[vmem()] * 3,
        scratch_shapes=[pltpu.VMEM(vector_shape, bf16), pltpu.VMEM((width, terms * width), bf16)],
        compiler_params=params(24),
        cost_estimate=work(4 * macs),
    )(
        plan,
        square,
        start_vector,
        units,
        far_units,
        lefts,
        rights,
    )
    got_tile = exchange(image_tiles[1], ZBIT)
    summed = kept + exchange(sent, CORE)
    first, second = pl.pallas_call(
        last_kernel,
        out_shape=[shaped(1, tile, tile)] * 2,
        in_specs=[smem()] + [vmem()] * 6,
        out_specs=[vmem()] * 2,
        compiler_params=params(4),
    )(
        plan,
        summed[0],
        exchange(summed[1].astype(bf16), XBIT),
        exchange(summed[2].astype(bf16), ZBIT),
        exchange(summed[3].astype(bf16), XBIT | ZBIT),
        image_tiles,
        got_tile,
    )
    return first, second


def solution(mesh):
    return jax.shard_map(
        on_device,
        mesh=mesh,
        in_specs=(
            P(("groups", "sec"), None, None),
            P(("groups", "sec"), None, None),
            P(("groups", "sec"), None, None),
            P(None, "groups"),
            P("groups"),
            P("groups", None),
            P("groups", None),
        ),
        out_specs=(P(("groups", "sec"), None, None), P(("groups", "sec"), None, None)),
        check_vma=False,
    )
```

```python
import jax
import jax.numpy as jnp
from jax import lax
from jax.experimental import pallas as pl
from jax.experimental.pallas import tpu as pltpu
from jax.sharding import PartitionSpec as P

GRID_ROWS = 4
GRID_COLS = 4
CORE, XBIT, YBIT, ZBIT = 1, 2, 4, 8
SECTOR_BIT = GRID_ROWS * GRID_COLS
EPSILON = 1e-06
EXTRA_ROWS = 16
MIB = 2**20
START_COST = 3
PEER_COST = 1
PLAN_BITS = 5


def exchange(block, flip):
    return lax.ppermute(block, "sec", [(i, i ^ flip) for i in range(lax.axis_size("sec"))])


def spread(tile, flip):
    route = []
    for i in range(lax.axis_size("sec")):
        x, z = i // XBIT % 2, i // ZBIT % 2
        new_x = x ^ z if flip >= SECTOR_BIT else z
        route.append((i, i + (new_x - x) * XBIT + (x - z) * ZBIT ^ flip))
    return lax.ppermute(tile, "sec", route)


def smem():
    return pl.BlockSpec(memory_space=pltpu.SMEM)


def vmem():
    return pl.BlockSpec(memory_space=pltpu.VMEM)


def anywhere():
    return pl.BlockSpec(memory_space=pl.ANY)


def live_block(sizes, row_start, col_start, shape):
    rows = row_start + lax.broadcasted_iota(jnp.int32, shape, 0)
    cols = col_start + lax.broadcasted_iota(jnp.int32, shape, 1)
    return (rows < sizes[0]) & (cols < sizes[1])


def term_of(plan, sectors, terms, k):
    base = PLAN_BITS + 2 * sectors
    return plan[base + k], plan[base + terms + k].astype(jnp.float32)


def mix(plan, sectors, terms, k, left, vector):
    source, weight = term_of(plan, sectors, terms, k)
    return jnp.dot(left, vector[source], preferred_element_type=jnp.float32) * weight


def put_pair(mixed, rows, k, pair):
    tile = pair[0].shape[1] // 2
    for half in range(2):
        at = slice(half * tile, (half + 1) * tile)
        both = jnp.concatenate([product[:, at] for product in pair], axis=1)
        mixed[half, rows, k * tile : (k + 2) * tile] = both.astype(jnp.bfloat16)


def collect(mixed, rights):
    terms, tile, width = rights.shape
    flat = rights[...].reshape(terms * tile, width)
    return jnp.dot(mixed, flat, preferred_element_type=jnp.float32)


def start_kernel(
    sectors, plan, near, far, left_own, right_own, vector, mixed_ref, square_ref, lefts, rights, sems
):
    terms, tile, _ = left_own.shape
    width = 2 * tile
    core, x, y, z = plan[0], plan[1], plan[2], plan[3]
    copies = [
        pltpu.make_async_copy(left_own, lefts, sems.at[0]),
        pltpu.make_async_copy(right_own, rights, sems.at[1]),
    ]
    for copy in copies:
        copy.start()
    square = jnp.zeros((8, width), jnp.float32)
    for xr in range(2):
        for yr in range(2):
            for sr in range(sectors):
                sector = plan[4] ^ sr
                z_row = x ^ xr ^ z if sr else x ^ xr
                row = (2 * z_row + (y ^ yr)) * tile
                sizes = plan[PLAN_BITS + 2 * sector], plan[PLAN_BITS + 2 * sector + 1]
                mine, other = near[xr, yr, sr], far[xr, yr, sr]
                low = jnp.where(core == 0, mine, other).astype(jnp.float32)
                high = jnp.where(core == 0, other, mine).astype(jnp.float32)
                top = jnp.concatenate([low[:, :tile], high[:, :tile]], axis=1)
                bottom = jnp.concatenate([low[:, tile:], high[:, tile:]], axis=1)
                both = jnp.concatenate([top, bottom], axis=0)
                both = jnp.where(live_block(sizes, row, z * width, both.shape), both, 0.0)
                square += jnp.sum((both * both).reshape(tile // 8, 8, width), axis=0)
                at = pl.ds(pl.multiple_of(row, tile), tile)
                vector[sector, at, :] = both.astype(jnp.bfloat16)
    square_ref[...] = jnp.broadcast_to(jnp.sum(square), square_ref.shape)
    copies[0].wait()
    for k in range(0, terms, 2):
        pair = [mix(plan, sectors, terms, i, lefts[i], vector) for i in (k, k + 1)]
        put_pair(mixed_ref, slice(None), k, pair)
    copies[1].wait()


def peer_kernel(
    sectors,
    plan,
    vector,
    mixed_own,
    left_own,
    left_peer,
    right_own,
    right_early,
    mixed_ref,
    total_ref,
    lefts,
    mixed,
    sems,
):
    terms, tile, _ = left_peer.shape
    early = right_early.shape[0] * tile
    y, z = plan[2], plan[3]
    own = pl.ds(pl.multiple_of(z * tile, tile), tile)
    peer = pl.ds(pl.multiple_of((1 - z) * tile, tile), tile)
    copies = [
        pltpu.make_async_copy(left_own, lefts.at[:, own], sems.at[0]),
        pltpu.make_async_copy(left_peer, lefts.at[:, peer], sems.at[1]),
    ]
    for copy in copies:
        copy.start()
    mixed[:, own, :] = mixed_own[...]
    for k in range(0, terms, 2):
        pair = [mix(plan, sectors, terms, i, left_peer[i], vector) for i in (k, k + 1)]
        put_pair(mixed, peer, k, pair)
    rest = mixed[1 - y]
    total_ref[...] = collect(mixed[y], right_own) + collect(rest[:, :early], right_early)
    mixed_ref[...] = rest[:, early:]
    for copy in copies:
        copy.wait()


def first_kernel(plan, mixed, before, right_own, right_early, right_late, kept_ref, sent_ref, rights, sems):
    early, tile, _ = right_early.shape
    late = right_late.shape[0]
    core, x, y, z = plan[0], plan[1], plan[2], plan[3]
    own = pl.ds(pl.multiple_of(y * tile, tile), tile)
    peer = pl.ds(pl.multiple_of((1 - y) * tile, tile), tile)
    copies = [
        pltpu.make_async_copy(right_own, rights.at[:, own], sems.at[0]),
        pltpu.make_async_copy(right_early, rights.at[pl.ds(0, early), peer], sems.at[1]),
        pltpu.make_async_copy(right_late, rights.at[pl.ds(early, late), peer], sems.at[2]),
    ]
    for copy in copies:
        copy.start()
    total = before[...] + collect(mixed[...], right_late)
    sizes = plan[PLAN_BITS + 2 * plan[4]], plan[PLAN_BITS + 2 * plan[4] + 1]
    parts = []
    for z_row in range(2):
        part = total[z_row * tile : (z_row + 1) * tile]
        keep = live_block(sizes, (2 * z_row + y) * tile, 0, part.shape)
        parts.append(jnp.where(keep, part, 0.0))
    _, unit_rows, unit_cols = kept_ref.shape
    for core_is in range(2):
        for x_is in range(2):
            for z_is in range(2):

                @pl.when((core == core_is) & (x == x_is) & (z == z_is))
                def _():
                    mine, other = parts[core_is], parts[1 - core_is]
                    for xr in range(2):
                        for zr in range(2):
                            row, col = (x_is ^ xr) * unit_rows, (z_is ^ zr) * unit_cols
                            at = slice(row, row + unit_rows), slice(col, col + unit_cols)
                            kept_ref[2 * zr + xr] = mine[at]
                            sent_ref[2 * zr + xr] = other[at]

    for copy in copies:
        copy.wait()


def second_kernel(
    sectors,
    plan,
    square_ref,
    start,
    near,
    far,
    lefts,
    rights,
    kept_ref,
    sent_ref,
    tiles_ref,
    vector,
    mixed,
):
    terms, width, _ = lefts.shape
    tile = width // 2
    half = tile // 2
    core, x, y, z = plan[0], plan[1], plan[2], plan[3]
    for pieces, z_row in ((near, core), (far, 1 - core)):
        for xr in range(2):
            for yr in range(2):
                for sr in range(sectors):
                    row = (2 * z_row + (y ^ yr)) * tile + (x ^ xr) * half
                    at = pl.ds(pl.multiple_of(row, half), half)
                    vector[plan[4] ^ sr, at, :] = pieces[2 * xr + yr, sr]
    inner = jnp.zeros((8, width), jnp.float32)
    norm = inner
    for k in range(terms):
        product = mix(plan, sectors, terms, k, lefts[k], vector)
        mixed[:, k * width : (k + 1) * width] = product.astype(jnp.bfloat16)
        if k < 4:
            for sr in range(sectors):
                row = (2 * core + (y ^ (k % 2))) * tile + (x ^ (k // 2)) * half
                at = pl.ds(pl.multiple_of(row, half), half)
                image = near[k, sr].astype(jnp.float32)
                before = start[plan[4] ^ sr, at, :].astype(jnp.float32)
                inner += jnp.sum((before * image).reshape(half // 8, 8, width), axis=0)
                norm += jnp.sum((image * image).reshape(half // 8, 8, width), axis=0)
    total = collect(mixed[...], rights)
    extra_shape = (EXTRA_ROWS, kept_ref.shape[2])
    lane = lax.broadcasted_iota(jnp.int32, extra_shape, 1)
    zeros = jnp.zeros(extra_shape, jnp.float32)
    own_sums, z_sums = zeros, zeros
    for k, value in enumerate((0.5 * square_ref[0, 0], jnp.sum(inner), jnp.sum(norm))):
        value = jnp.broadcast_to(value, extra_shape)
        own_sums = jnp.where(lane == k, value, own_sums)
        for level in range(3):
            piece = value.astype(jnp.bfloat16).astype(jnp.float32)
            z_sums = jnp.where(lane == 9 * core + 3 * k + level, piece, z_sums)
            value = value - piece

    def packed(block, row, col):
        halves = [block[row + r : row + r + half, col : col + tile] for r in (0, half)]
        return jnp.concatenate(halves, axis=1)

    image_tiles = []
    for z_row in (z, 1 - z):
        row = pl.multiple_of((2 * z_row + y) * tile, tile)
        image_tiles.append(vector[plan[4], pl.ds(row, tile), :].astype(jnp.float32))
    for core_is in range(2):

        @pl.when(core == core_is)
        def _():
            for k in range(2):
                tiles_ref[k] = packed(image_tiles[k], 0, core_is * tile).astype(tiles_ref.dtype)

        for x_is in range(2):
            for z_is in range(2):

                @pl.when((core == core_is) & (x == x_is) & (z == z_is))
                def _():
                    for xr in range(2):
                        for zr in range(2):
                            row = (z_is ^ zr) * tile
                            col = (x_is ^ xr) * width
                            mine = packed(total, row, col + core_is * tile)
                            other = packed(total, row, col + (1 - core_is) * tile)
                            kept_ref[2 * zr + xr, :half] = mine
                            sent_ref[2 * zr + xr, :half] = other

    for to in range(4):
        kept_ref[to, half:] = (own_sums, zeros, z_sums, zeros)[to]
        sent_ref[to, half:] = (own_sums, zeros, z_sums, zeros)[to]


def last_kernel(plan, own_ref, from_x, from_z, from_xz, tiles_ref, got_ref, first_ref, out_ref):
    _, rows, cols = out_ref.shape
    half = rows // 2
    core, x, y, z, sector = plan[0], plan[1], plan[2], plan[3], plan[4]
    total = own_ref[:half] + from_x[:half].astype(jnp.float32)
    total += from_z[:half].astype(jnp.float32) + from_xz[:half].astype(jnp.float32)
    own_sums = own_ref[half : half + 8]
    z_sums = from_z[half : half + EXTRA_ROWS].astype(jnp.float32)[:8]
    image = jnp.where(x == z, tiles_ref[0], got_ref[...]).astype(jnp.float32)
    lane = lax.broadcasted_iota(jnp.int32, own_sums.shape, 1)

    def pick(values, wanted):
        return jnp.sum(jnp.where(wanted, values, 0.0), axis=1, keepdims=True)[:1]

    sums = []
    for k in range(3):
        z_part = pick(z_sums, (lane % 9 // 3 == k) & (lane < 18))
        sums.append(pick(own_sums, lane == k) + z_part)
    square, inner, norm = sums
    quotient = inner / square
    residual_square = jnp.maximum(norm - quotient * inner, 0.0)
    scale = lax.rsqrt(residual_square / square + EPSILON)
    sizes = plan[PLAN_BITS + 2 * sector], plan[PLAN_BITS + 2 * sector + 1]
    second = (total - quotient * image) * scale
    for k in range(2):
        at = slice(k * half, (k + 1) * half)
        part = slice(k * cols, (k + 1) * cols)
        first_ref[0, at] = image[:, part].astype(jnp.bfloat16)
        row = (2 * z + y) * rows + k * half
        keep = live_block(sizes, row, (2 * x + core) * cols, (half, cols))
        out_ref[0, at] = jnp.where(keep, second[:, part], 0.0).astype(jnp.bfloat16)


def on_device(
    wavefunction, left_environment, right_environment, sector_sizes, pairing, term_mask, coupling
):
    tile = wavefunction.shape[1]
    terms = left_environment.shape[0]
    sectors = lax.axis_size("sec") // SECTOR_BIT
    capacity = tile * GRID_ROWS
    bf16, f32 = jnp.bfloat16, jnp.float32

    def shaped(*shape, dtype=bf16):
        return jax.ShapeDtypeStruct(shape, dtype)

    index = lax.axis_index("sec").astype(jnp.int32)
    bits = [index % 2, index // XBIT % 2, index // YBIT % 2, index // ZBIT % 2, index // SECTOR_BIT]
    sizes = jnp.stack([sector_sizes[0], jnp.take(sector_sizes[1], pairing)], axis=1)
    group = index % GRID_COLS * terms

    def mine(table):
        row = lax.dynamic_slice(table, (bits[4], group), (1, terms))
        return row.reshape(terms)

    plan = jnp.concatenate([jnp.stack(bits), sizes.reshape(-1), mine(coupling), mine(term_mask)])

    start_tile = jnp.concatenate([wavefunction[0, : tile // 2], wavefunction[0, tile // 2 :]], axis=1)
    early = terms // 6
    tiles = [spread(start_tile, flip) for flip in range(0, lax.axis_size("sec"), SECTOR_BIT)]
    gated, tiles[0] = lax.optimization_barrier((left_environment, tiles[0]))
    tiles = jnp.stack(tiles)
    tiles = jnp.stack([tiles, exchange(tiles, YBIT)])
    right_early = exchange(right_environment[:early], YBIT)
    tiles, right_early = lax.optimization_barrier((tiles, right_early))
    tiles = jnp.stack([tiles, exchange(tiles, XBIT)])
    far_tiles = exchange(tiles, CORE)

    left_peer = exchange(gated, ZBIT)
    right_late = exchange(right_environment[early:], YBIT)

    def work(macs):
        return pl.CostEstimate(flops=int(2 * macs), bytes_accessed=terms * tile * capacity * 4, transcendentals=0)

    width = 2 * tile
    macs = terms * tile * capacity * width
    vector_shape = (sectors, capacity, width)
    unit = (4, tile // 2, width)

    def params(mib):
        return pltpu.CompilerParams(vmem_limit_bytes=mib * MIB)

    start_vector, mixed_own, square, left_own, right_own = pl.pallas_call(
        lambda *refs: start_kernel(sectors, *refs),
        out_shape=[
            shaped(*vector_shape),
            shaped(2, tile, terms * tile),
            shaped(8, 128, dtype=f32),
            shaped(terms, tile, capacity),
            shaped(terms, tile, capacity),
        ],
        in_specs=[smem(), vmem(), vmem(), anywhere(), anywhere()],
        out_specs=[vmem()] * 5,
        scratch_shapes=[pltpu.SemaphoreType.DMA((2,))],
        compiler_params=params(16),
        cost_estimate=work(START_COST * macs),
    )(plan, tiles, far_tiles, left_environment, right_environment)
    mixed, total, lefts = pl.pallas_call(
        lambda *refs: peer_kernel(sectors, *refs),
        out_shape=[
            shaped(width, (terms - early) * tile),
            shaped(width, capacity, dtype=f32),
            shaped(terms, width, capacity),
        ],
        in_specs=[smem()] + [vmem()] * 6,
        out_specs=[vmem()] * 3,
        scratch_shapes=[pltpu.VMEM((2, width, terms * tile), bf16), pltpu.SemaphoreType.DMA((2,))],
        compiler_params=params(20),
        cost_estimate=work(PEER_COST * macs),
    )(plan, start_vector, mixed_own, left_own, left_peer, right_own, right_early)
    kept, sent, rights = pl.pallas_call(
        first_kernel,
        out_shape=[shaped(*unit, dtype=f32)] * 2 + [shaped(terms, width, capacity)],
        in_specs=[smem()] + [vmem()] * 5,
        out_specs=[vmem()] * 3,
        scratch_shapes=[pltpu.SemaphoreType.DMA((3,))],
        compiler_params=params(16),
        cost_estimate=work(macs),
    )(plan, mixed, total, right_own, right_early, right_late)

    summed = kept + exchange(sent, CORE)
    image_unit = (
        summed[0]
        + exchange(summed[1].astype(bf16), XBIT).astype(f32)
        + exchange(summed[2].astype(bf16), ZBIT).astype(f32)
        + exchange(summed[3].astype(bf16), XBIT | ZBIT).astype(f32)
    )
    units = image_unit.astype(bf16)[None]
    flip = SECTOR_BIT
    while flip < lax.axis_size("sec"):
        units = jnp.concatenate([units, exchange(units, flip)])
        flip *= 2
    units = jnp.stack(
        [units, exchange(units, YBIT), exchange(units, XBIT), exchange(units, XBIT | YBIT)]
    )
    far_units = exchange(units, CORE)
    half = tile // 2
    part = (4, half + EXTRA_ROWS, width)
    kept, sent, image_tiles = pl.pallas_call(
        lambda *refs: second_kernel(sectors, *refs),
        out_shape=[shaped(*part, dtype=f32)] * 2 + [shaped(2, half, width)],
        in_specs=[smem()] + [vmem()] * 6,
        out_specs=[vmem()] * 3,
        scratch_shapes=[pltpu.VMEM(vector_shape, bf16), pltpu.VMEM((width, terms * width), bf16)],
        compiler_params=params(24),
        cost_estimate=work(4 * macs),
    )(
        plan,
        square,
        start_vector,
        units,
        far_units,
        lefts,
        rights,
    )
    got_tile = exchange(image_tiles[1], ZBIT)
    summed = kept + exchange(sent, CORE)
    first, second = pl.pallas_call(
        last_kernel,
        out_shape=[shaped(1, tile, tile)] * 2,
        in_specs=[smem()] + [vmem()] * 6,
        out_specs=[vmem()] * 2,
        compiler_params=params(4),
    )(
        plan,
        summed[0],
        exchange(summed[1].astype(bf16), XBIT),
        exchange(summed[2].astype(bf16), ZBIT),
        exchange(summed[3].astype(bf16), XBIT | ZBIT),
        image_tiles,
        got_tile,
    )
    return first, second


def solution(mesh):
    return jax.shard_map(
        on_device,
        mesh=mesh,
        in_specs=(
            P(("groups", "sec"), None, None),
            P(("groups", "sec"), None, None),
            P(("groups", "sec"), None, None),
            P(None, "groups"),
            P("groups"),
            P("groups", None),
            P("groups", None),
        ),
        out_specs=(P(("groups", "sec"), None, None), P(("groups", "sec"), None, None)),
        check_vma=False,
    )
```

```python
import jax
import jax.numpy as jnp
from jax import lax
from jax.experimental import pallas as pl
from jax.experimental.pallas import tpu as pltpu
from jax.sharding import PartitionSpec as P

GRID_ROWS = 4
GRID_COLS = 4
CORE, XBIT, YBIT, ZBIT = 1, 2, 4, 8
SECTOR_BIT = GRID_ROWS * GRID_COLS
EPSILON = 1e-06
EXTRA_ROWS = 16
MIB = 2**20
START_COST = 3
PEER_COST = 1
PEER_MIB = 16
PLAN_BITS = 5


def exchange(block, flip):
    return lax.ppermute(block, "sec", [(i, i ^ flip) for i in range(lax.axis_size("sec"))])


def spread(tile, flip):
    route = []
    for i in range(lax.axis_size("sec")):
        x, z = i // XBIT % 2, i // ZBIT % 2
        new_x = x ^ z if flip >= SECTOR_BIT else z
        route.append((i, i + (new_x - x) * XBIT + (x - z) * ZBIT ^ flip))
    return lax.ppermute(tile, "sec", route)


def smem():
    return pl.BlockSpec(memory_space=pltpu.SMEM)


def vmem():
    return pl.BlockSpec(memory_space=pltpu.VMEM)


def anywhere():
    return pl.BlockSpec(memory_space=pl.ANY)


def live_block(sizes, row_start, col_start, shape):
    rows = row_start + lax.broadcasted_iota(jnp.int32, shape, 0)
    cols = col_start + lax.broadcasted_iota(jnp.int32, shape, 1)
    return (rows < sizes[0]) & (cols < sizes[1])


def term_of(plan, sectors, terms, k):
    base = PLAN_BITS + 2 * sectors
    return plan[base + k], plan[base + terms + k].astype(jnp.float32)


def mix(plan, sectors, terms, k, left, vector):
    source, weight = term_of(plan, sectors, terms, k)
    return jnp.dot(left, vector[source], preferred_element_type=jnp.float32) * weight


def put_pair(mixed, k, pair):
    tile = pair[0].shape[1] // 2
    for half in range(2):
        at = slice(half * tile, (half + 1) * tile)
        both = jnp.concatenate([product[:, at] for product in pair], axis=1)
        mixed[half, :, k * tile : (k + 2) * tile] = both.astype(jnp.bfloat16)


def collect(mixed, rights):
    terms, tile, width = rights.shape
    flat = rights[...].reshape(terms * tile, width)
    return jnp.dot(mixed, flat, preferred_element_type=jnp.float32)


def start_kernel(
    sectors,
    plan,
    near,
    far,
    left_own,
    right_own,
    right_early,
    vector,
    mixed_ref,
    total_ref,
    square_ref,
    lefts,
    rights,
    sems,
):
    terms, tile, _ = left_own.shape
    early = right_early.shape[0] * tile
    width = 2 * tile
    core, x, y, z = plan[0], plan[1], plan[2], plan[3]
    copies = [
        pltpu.make_async_copy(left_own, lefts, sems.at[0]),
        pltpu.make_async_copy(right_own, rights, sems.at[1]),
    ]
    for copy in copies:
        copy.start()
    square = jnp.zeros((8, width), jnp.float32)
    for xr in range(2):
        for yr in range(2):
            for sr in range(sectors):
                sector = plan[4] ^ sr
                z_row = x ^ xr ^ z if sr else x ^ xr
                row = (2 * z_row + (y ^ yr)) * tile
                sizes = plan[PLAN_BITS + 2 * sector], plan[PLAN_BITS + 2 * sector + 1]
                mine, other = near[xr, yr, sr], far[xr, yr, sr]
                low = jnp.where(core == 0, mine, other).astype(jnp.float32)
                high = jnp.where(core == 0, other, mine).astype(jnp.float32)
                top = jnp.concatenate([low[:, :tile], high[:, :tile]], axis=1)
                bottom = jnp.concatenate([low[:, tile:], high[:, tile:]], axis=1)
                both = jnp.concatenate([top, bottom], axis=0)
                both = jnp.where(live_block(sizes, row, z * width, both.shape), both, 0.0)
                square += jnp.sum((both * both).reshape(tile // 8, 8, width), axis=0)
                at = pl.ds(pl.multiple_of(row, tile), tile)
                vector[sector, at, :] = both.astype(jnp.bfloat16)
    square_ref[...] = jnp.broadcast_to(jnp.sum(square), square_ref.shape)
    copies[0].wait()
    for k in range(0, terms, 2):
        pair = [mix(plan, sectors, terms, i, lefts[i], vector) for i in (k, k + 1)]
        put_pair(mixed_ref, k, pair)
    copies[1].wait()
    total = collect(mixed_ref[y], rights)
    total_ref[...] = total + collect(mixed_ref[1 - y][:, :early], right_early)


def peer_kernel(
    sectors,
    plan,
    vector,
    left_own,
    left_peer,
    right_own,
    right_early,
    mixed,
    total_ref,
    lefts,
    sems,
):
    terms, tile, _ = left_peer.shape
    early = right_early.shape[0] * tile
    y, z = plan[2], plan[3]
    own = pl.ds(pl.multiple_of(z * tile, tile), tile)
    peer = pl.ds(pl.multiple_of((1 - z) * tile, tile), tile)
    copies = [
        pltpu.make_async_copy(left_own, lefts.at[:, own], sems.at[0]),
        pltpu.make_async_copy(left_peer, lefts.at[:, peer], sems.at[1]),
    ]
    for copy in copies:
        copy.start()
    for k in range(0, terms, 2):
        pair = [mix(plan, sectors, terms, i, left_peer[i], vector) for i in (k, k + 1)]
        put_pair(mixed, k, pair)
    total_ref[...] = collect(mixed[y], right_own) + collect(mixed[1 - y][:, :early], right_early)
    for copy in copies:
        copy.wait()


def first_kernel(
    plan,
    mixed_own,
    mixed_peer,
    before_own,
    before_peer,
    right_own,
    right_early,
    right_late,
    kept_ref,
    sent_ref,
    rights,
    parts,
    sems,
):
    early, tile, _ = right_early.shape
    late = right_late.shape[0]
    core, x, y, z = plan[0], plan[1], plan[2], plan[3]
    own = pl.ds(pl.multiple_of(y * tile, tile), tile)
    peer = pl.ds(pl.multiple_of((1 - y) * tile, tile), tile)
    copies = [
        pltpu.make_async_copy(right_own, rights.at[:, own], sems.at[0]),
        pltpu.make_async_copy(right_early, rights.at[pl.ds(0, early), peer], sems.at[1]),
        pltpu.make_async_copy(right_late, rights.at[pl.ds(early, late), peer], sems.at[2]),
    ]
    for copy in copies:
        copy.start()
    sizes = plan[PLAN_BITS + 2 * plan[4]], plan[PLAN_BITS + 2 * plan[4] + 1]
    for k, (mixed, before, z_row) in enumerate(
        ((mixed_own, before_own, z), (mixed_peer, before_peer, 1 - z))
    ):
        part = before[...] + collect(mixed[1 - y][:, early * tile :], right_late)
        keep = live_block(sizes, (2 * z_row + y) * tile, 0, part.shape)
        parts[k] = jnp.where(keep, part, 0.0)
    _, unit_rows, unit_cols = kept_ref.shape
    for xr in range(2):
        for zr in range(2):
            at = (
                pl.ds(pl.multiple_of((x ^ xr) * unit_rows, unit_rows), unit_rows),
                pl.ds(pl.multiple_of((z ^ zr) * unit_cols, unit_cols), unit_cols),
            )
            kept_ref[2 * zr + xr] = parts[(core ^ z, *at)]
            sent_ref[2 * zr + xr] = parts[(1 - (core ^ z), *at)]
    for copy in copies:
        copy.wait()


def second_kernel(
    sectors,
    plan,
    square_ref,
    start,
    near,
    far,
    lefts,
    rights,
    kept_ref,
    sent_ref,
    tiles_ref,
    vector,
    mixed,
    total,
):
    terms, width, _ = lefts.shape
    tile = width // 2
    half = tile // 2
    core, x, y, z = plan[0], plan[1], plan[2], plan[3]
    for pieces, z_row in ((near, core), (far, 1 - core)):
        for xr in range(2):
            for yr in range(2):
                for sr in range(sectors):
                    row = (2 * z_row + (y ^ yr)) * tile + (x ^ xr) * half
                    at = pl.ds(pl.multiple_of(row, half), half)
                    vector[plan[4] ^ sr, at, :] = pieces[2 * xr + yr, sr]
    inner = jnp.zeros((8, width), jnp.float32)
    norm = inner
    for k in range(terms):
        product = mix(plan, sectors, terms, k, lefts[k], vector)
        mixed[:, k * width : (k + 1) * width] = product.astype(jnp.bfloat16)
        if k < 4:
            for sr in range(sectors):
                row = (2 * core + (y ^ (k % 2))) * tile + (x ^ (k // 2)) * half
                at = pl.ds(pl.multiple_of(row, half), half)
                image = near[k, sr].astype(jnp.float32)
                before = start[plan[4] ^ sr, at, :].astype(jnp.float32)
                inner += jnp.sum((before * image).reshape(half // 8, 8, width), axis=0)
                norm += jnp.sum((image * image).reshape(half // 8, 8, width), axis=0)
    total[...] = collect(mixed[...], rights)
    extra_shape = (EXTRA_ROWS, kept_ref.shape[2])
    lane = lax.broadcasted_iota(jnp.int32, extra_shape, 1)
    zeros = jnp.zeros(extra_shape, jnp.float32)
    own_sums, z_sums = zeros, zeros
    for k, value in enumerate((0.5 * square_ref[0, 0], jnp.sum(inner), jnp.sum(norm))):
        value = jnp.broadcast_to(value, extra_shape)
        own_sums = jnp.where(lane == k, value, own_sums)
        for level in range(3):
            piece = value.astype(jnp.bfloat16).astype(jnp.float32)
            z_sums = jnp.where(lane == 9 * core + 3 * k + level, piece, z_sums)
            value = value - piece

    def packed(block):
        halves = []
        for col in (0, tile):
            parts = [block[row : row + half, col : col + tile] for row in (0, half)]
            halves.append(jnp.concatenate(parts, axis=1))
        return jnp.where(core == 0, halves[0], halves[1]), jnp.where(core == 0, halves[1], halves[0])

    for k, z_row in enumerate((z, 1 - z)):
        row = pl.multiple_of((2 * z_row + y) * tile, tile)
        image = vector[plan[4], pl.ds(row, tile), :].astype(jnp.float32)
        tiles_ref[k] = packed(image)[0].astype(tiles_ref.dtype)
    for xr in range(2):
        for zr in range(2):
            at = (
                pl.ds(pl.multiple_of((z ^ zr) * tile, tile), tile),
                pl.ds(pl.multiple_of((x ^ xr) * width, width), width),
            )
            mine, other = packed(total[at])
            kept_ref[2 * zr + xr, :half] = mine
            sent_ref[2 * zr + xr, :half] = other
    for to in range(4):
        kept_ref[to, half:] = (own_sums, zeros, z_sums, zeros)[to]
        sent_ref[to, half:] = (own_sums, zeros, z_sums, zeros)[to]


def last_kernel(plan, own_ref, from_x, from_z, from_xz, tiles_ref, got_ref, first_ref, out_ref):
    _, rows, cols = out_ref.shape
    half = rows // 2
    core, x, y, z, sector = plan[0], plan[1], plan[2], plan[3], plan[4]
    total = own_ref[:half] + from_x[:half].astype(jnp.float32)
    total += from_z[:half].astype(jnp.float32) + from_xz[:half].astype(jnp.float32)
    own_sums = own_ref[half : half + 8]
    z_sums = from_z[half : half + EXTRA_ROWS].astype(jnp.float32)[:8]
    image = jnp.where(x == z, tiles_ref[0], got_ref[...]).astype(jnp.float32)
    lane = lax.broadcasted_iota(jnp.int32, own_sums.shape, 1)

    def pick(values, wanted):
        return jnp.sum(jnp.where(wanted, values, 0.0), axis=1, keepdims=True)[:1]

    sums = []
    for k in range(3):
        z_part = pick(z_sums, (lane % 9 // 3 == k) & (lane < 18))
        sums.append(pick(own_sums, lane == k) + z_part)
    square, inner, norm = sums
    quotient = inner / square
    residual_square = jnp.maximum(norm - quotient * inner, 0.0)
    scale = lax.rsqrt(residual_square / square + EPSILON)
    sizes = plan[PLAN_BITS + 2 * sector], plan[PLAN_BITS + 2 * sector + 1]
    second = (total - quotient * image) * scale
    for k in range(2):
        at = slice(k * half, (k + 1) * half)
        part = slice(k * cols, (k + 1) * cols)
        first_ref[0, at] = image[:, part].astype(jnp.bfloat16)
        row = (2 * z + y) * rows + k * half
        keep = live_block(sizes, row, (2 * x + core) * cols, (half, cols))
        out_ref[0, at] = jnp.where(keep, second[:, part], 0.0).astype(jnp.bfloat16)


def on_device(
    wavefunction, left_environment, right_environment, sector_sizes, pairing, term_mask, coupling
):
    tile = wavefunction.shape[1]
    terms = left_environment.shape[0]
    sectors = lax.axis_size("sec") // SECTOR_BIT
    capacity = tile * GRID_ROWS
    bf16, f32 = jnp.bfloat16, jnp.float32

    def shaped(*shape, dtype=bf16):
        return jax.ShapeDtypeStruct(shape, dtype)

    index = lax.axis_index("sec").astype(jnp.int32)
    bits = [index % 2, index // XBIT % 2, index // YBIT % 2, index // ZBIT % 2, index // SECTOR_BIT]
    sizes = jnp.stack([sector_sizes[0], jnp.take(sector_sizes[1], pairing)], axis=1)
    group = index % GRID_COLS * terms

    def mine(table):
        row = lax.dynamic_slice(table, (bits[4], group), (1, terms))
        return row.reshape(terms)

    plan = jnp.concatenate([jnp.stack(bits), sizes.reshape(-1), mine(coupling), mine(term_mask)])

    start_tile = jnp.concatenate([wavefunction[0, : tile // 2], wavefunction[0, tile // 2 :]], axis=1)
    early = terms // 6
    tiles = [spread(start_tile, flip) for flip in range(0, lax.axis_size("sec"), SECTOR_BIT)]
    gated, tiles[0] = lax.optimization_barrier((left_environment, tiles[0]))
    tiles = jnp.stack(tiles)
    tiles = jnp.stack([tiles, exchange(tiles, YBIT)])
    right_early = exchange(right_environment[:early], YBIT)
    tiles, right_early = lax.optimization_barrier((tiles, right_early))
    tiles = jnp.stack([tiles, exchange(tiles, XBIT)])
    far_tiles = exchange(tiles, CORE)

    left_peer = exchange(gated, ZBIT)
    right_late = exchange(right_environment[early:], YBIT)

    def work(macs):
        return pl.CostEstimate(flops=int(2 * macs), bytes_accessed=terms * tile * capacity * 4, transcendentals=0)

    width = 2 * tile
    macs = terms * tile * capacity * width
    vector_shape = (sectors, capacity, width)
    unit = (4, tile // 2, width)

    def params(mib):
        return pltpu.CompilerParams(vmem_limit_bytes=mib * MIB)

    total_shape = shaped(tile, capacity, dtype=f32)
    mixed_shape = shaped(2, tile, terms * tile)
    start_vector, mixed_own, total_own, square, left_own, right_own = pl.pallas_call(
        lambda *refs: start_kernel(sectors, *refs),
        out_shape=[
            shaped(*vector_shape),
            mixed_shape,
            total_shape,
            shaped(8, 128, dtype=f32),
            shaped(terms, tile, capacity),
            shaped(terms, tile, capacity),
        ],
        in_specs=[smem(), vmem(), vmem(), anywhere(), anywhere(), vmem()],
        out_specs=[vmem()] * 6,
        scratch_shapes=[pltpu.SemaphoreType.DMA((2,))],
        compiler_params=params(16),
        cost_estimate=work(START_COST * macs),
    )(plan, tiles, far_tiles, left_environment, right_environment, right_early)
    mixed_peer, total_peer, lefts = pl.pallas_call(
        lambda *refs: peer_kernel(sectors, *refs),
        out_shape=[mixed_shape, total_shape, shaped(terms, width, capacity)],
        in_specs=[smem()] + [vmem()] * 5,
        out_specs=[vmem()] * 3,
        scratch_shapes=[pltpu.SemaphoreType.DMA((2,))],
        compiler_params=params(PEER_MIB),
        cost_estimate=work(PEER_COST * macs),
    )(plan, start_vector, left_own, left_peer, right_own, right_early)
    kept, sent, rights = pl.pallas_call(
        first_kernel,
        out_shape=[shaped(*unit, dtype=f32)] * 2 + [shaped(terms, width, capacity)],
        in_specs=[smem()] + [vmem()] * 7,
        out_specs=[vmem()] * 3,
        scratch_shapes=[pltpu.VMEM((2, tile, capacity), f32), pltpu.SemaphoreType.DMA((3,))],
        compiler_params=params(16),
        cost_estimate=work(macs),
    )(plan, mixed_own, mixed_peer, total_own, total_peer, right_own, right_early, right_late)

    summed = kept + exchange(sent, CORE)
    image_unit = (
        summed[0]
        + exchange(summed[1].astype(bf16), XBIT).astype(f32)
        + exchange(summed[2].astype(bf16), ZBIT).astype(f32)
        + exchange(summed[3].astype(bf16), XBIT | ZBIT).astype(f32)
    )
    units = image_unit.astype(bf16)[None]
    flip = SECTOR_BIT
    while flip < lax.axis_size("sec"):
        units = jnp.concatenate([units, exchange(units, flip)])
        flip *= 2
    units = jnp.stack(
        [units, exchange(units, YBIT), exchange(units, XBIT), exchange(units, XBIT | YBIT)]
    )
    far_units = exchange(units, CORE)
    half = tile // 2
    part = (4, half + EXTRA_ROWS, width)
    kept, sent, image_tiles = pl.pallas_call(
        lambda *refs: second_kernel(sectors, *refs),
        out_shape=[shaped(*part, dtype=f32)] * 2 + [shaped(2, half, width)],
        in_specs=[smem()] + [vmem()] * 6,
        out_specs=[vmem()] * 3,
        scratch_shapes=[
            pltpu.VMEM(vector_shape, bf16),
            pltpu.VMEM((width, terms * width), bf16),
            pltpu.VMEM((width, capacity), f32),
        ],
        compiler_params=params(24),
        cost_estimate=work(4 * macs),
    )(
        plan,
        square,
        start_vector,
        units,
        far_units,
        lefts,
        rights,
    )
    got_tile = exchange(image_tiles[1], ZBIT)
    summed = kept + exchange(sent, CORE)
    first, second = pl.pallas_call(
        last_kernel,
        out_shape=[shaped(1, tile, tile)] * 2,
        in_specs=[smem()] + [vmem()] * 6,
        out_specs=[vmem()] * 2,
        compiler_params=params(4),
    )(
        plan,
        summed[0],
        exchange(summed[1].astype(bf16), XBIT),
        exchange(summed[2].astype(bf16), ZBIT),
        exchange(summed[3].astype(bf16), XBIT | ZBIT),
        image_tiles,
        got_tile,
    )
    return first, second


def solution(mesh):
    return jax.shard_map(
        on_device,
        mesh=mesh,
        in_specs=(
            P(("groups", "sec"), None, None),
            P(("groups", "sec"), None, None),
            P(("groups", "sec"), None, None),
            P(None, "groups"),
            P("groups"),
            P("groups", None),
            P("groups", None),
        ),
        out_specs=(P(("groups", "sec"), None, None), P(("groups", "sec"), None, None)),
        check_vma=False,
    )
```

```python
import jax
import jax.numpy as jnp
from jax import lax
from jax.experimental import pallas as pl
from jax.experimental.pallas import tpu as pltpu
from jax.sharding import PartitionSpec as P

GRID_ROWS = 4
GRID_COLS = 4
CORE, XBIT, YBIT, ZBIT = 1, 2, 4, 8
SECTOR_BIT = GRID_ROWS * GRID_COLS
EPSILON = 1e-06
EXTRA_ROWS = 16
MIB = 2**20
START_COST = 3
PEER_COST = 1
PEER_MIB = 16
PLAN_BITS = 5


def exchange(block, flip):
    return lax.ppermute(block, "sec", [(i, i ^ flip) for i in range(lax.axis_size("sec"))])


def spread(tile, flip):
    route = []
    for i in range(lax.axis_size("sec")):
        x, z = i // XBIT % 2, i // ZBIT % 2
        new_x = x ^ z if flip >= SECTOR_BIT else z
        route.append((i, i + (new_x - x) * XBIT + (x - z) * ZBIT ^ flip))
    return lax.ppermute(tile, "sec", route)


def smem():
    return pl.BlockSpec(memory_space=pltpu.SMEM)


def vmem():
    return pl.BlockSpec(memory_space=pltpu.VMEM)


def anywhere():
    return pl.BlockSpec(memory_space=pl.ANY)


def live_block(sizes, row_start, col_start, shape):
    rows = row_start + lax.broadcasted_iota(jnp.int32, shape, 0)
    cols = col_start + lax.broadcasted_iota(jnp.int32, shape, 1)
    return (rows < sizes[0]) & (cols < sizes[1])


def term_of(plan, sectors, terms, k):
    base = PLAN_BITS + 2 * sectors
    return plan[base + k], plan[base + terms + k].astype(jnp.float32)


def mix(plan, sectors, terms, k, left, vector):
    source, weight = term_of(plan, sectors, terms, k)
    return jnp.dot(left, vector[source], preferred_element_type=jnp.float32) * weight


def put_pair(mixed, k, pair):
    tile = pair[0].shape[1] // 2
    for half in range(2):
        at = slice(half * tile, (half + 1) * tile)
        both = jnp.concatenate([product[:, at] for product in pair], axis=1)
        mixed[half, :, k * tile : (k + 2) * tile] = both.astype(jnp.bfloat16)


def collect(mixed, rights):
    terms, tile, width = rights.shape
    flat = rights[...].reshape(terms * tile, width)
    return jnp.dot(mixed, flat, preferred_element_type=jnp.float32)


def start_kernel(
    sectors,
    plan,
    near,
    far,
    left_own,
    right_own,
    right_early,
    vector,
    mixed_ref,
    total_ref,
    square_ref,
    lefts,
    rights,
    sems,
):
    terms, tile, _ = left_own.shape
    early = right_early.shape[0] * tile
    width = 2 * tile
    core, x, y, z = plan[0], plan[1], plan[2], plan[3]
    copies = [
        pltpu.make_async_copy(left_own, lefts, sems.at[0]),
        pltpu.make_async_copy(right_own, rights, sems.at[1]),
    ]
    for copy in copies:
        copy.start()
    square = jnp.zeros((8, width), jnp.float32)
    for xr in range(2):
        for yr in range(2):
            for sr in range(sectors):
                sector = plan[4] ^ sr
                z_row = x ^ xr ^ z if sr else x ^ xr
                row = (2 * z_row + (y ^ yr)) * tile
                sizes = plan[PLAN_BITS + 2 * sector], plan[PLAN_BITS + 2 * sector + 1]
                mine, other = near[xr, yr, sr], far[xr, yr, sr]
                low = jnp.where(core == 0, mine, other).astype(jnp.float32)
                high = jnp.where(core == 0, other, mine).astype(jnp.float32)
                top = jnp.concatenate([low[:, :tile], high[:, :tile]], axis=1)
                bottom = jnp.concatenate([low[:, tile:], high[:, tile:]], axis=1)
                both = jnp.concatenate([top, bottom], axis=0)
                both = jnp.where(live_block(sizes, row, z * width, both.shape), both, 0.0)
                square += jnp.sum((both * both).reshape(tile // 8, 8, width), axis=0)
                at = pl.ds(pl.multiple_of(row, tile), tile)
                vector[sector, at, :] = both.astype(jnp.bfloat16)
    square_ref[...] = jnp.broadcast_to(jnp.sum(square), square_ref.shape)
    copies[0].wait()
    for k in range(0, terms, 2):
        pair = [mix(plan, sectors, terms, i, lefts[i], vector) for i in (k, k + 1)]
        put_pair(mixed_ref, k, pair)
    copies[1].wait()
    total = collect(mixed_ref[y], rights)
    total_ref[...] = total + collect(mixed_ref[1 - y][:, :early], right_early)


def peer_kernel(
    sectors,
    plan,
    vector,
    left_own,
    left_peer,
    right_own,
    right_early,
    mixed,
    total_ref,
    lefts,
    sems,
):
    terms, tile, _ = left_peer.shape
    early = right_early.shape[0] * tile
    y, z = plan[2], plan[3]
    own = pl.ds(pl.multiple_of(z * tile, tile), tile)
    peer = pl.ds(pl.multiple_of((1 - z) * tile, tile), tile)
    copies = [
        pltpu.make_async_copy(left_own, lefts.at[:, own], sems.at[0]),
        pltpu.make_async_copy(left_peer, lefts.at[:, peer], sems.at[1]),
    ]
    for copy in copies:
        copy.start()
    for k in range(0, terms, 2):
        pair = [mix(plan, sectors, terms, i, left_peer[i], vector) for i in (k, k + 1)]
        put_pair(mixed, k, pair)
    total_ref[...] = collect(mixed[y], right_own) + collect(mixed[1 - y][:, :early], right_early)
    for copy in copies:
        copy.wait()


def finish_rows(plan, mine, rows, right_late, unit_ref, scratch):
    late, tile, _ = right_late.shape
    x, y, z = plan[1], plan[2], plan[3]
    (mixed_own, before_own), (mixed_peer, before_peer) = rows
    is_own = mine == z
    first = mixed_own.shape[2] - late * tile
    mixed = jnp.where(is_own, mixed_own[1 - y], mixed_peer[1 - y])[:, first:]
    total = jnp.where(is_own, before_own[...], before_peer[...]) + collect(mixed, right_late)
    sizes = plan[PLAN_BITS + 2 * plan[4]], plan[PLAN_BITS + 2 * plan[4] + 1]
    keep = live_block(sizes, (2 * mine + y) * tile, 0, total.shape)
    scratch[...] = jnp.where(keep, total, 0.0)
    _, unit_rows, unit_cols = unit_ref.shape
    for xr in range(2):
        for zr in range(2):
            at = (
                pl.ds(pl.multiple_of((x ^ xr) * unit_rows, unit_rows), unit_rows),
                pl.ds(pl.multiple_of((z ^ zr) * unit_cols, unit_cols), unit_cols),
            )
            unit_ref[2 * zr + xr] = scratch[at]


def sent_kernel(
    plan, mixed_own, mixed_peer, before_own, before_peer, right_late, sent_ref, late_ref, scratch, sem
):
    copy = pltpu.make_async_copy(right_late, late_ref, sem)
    copy.start()
    rows = ((mixed_own, before_own), (mixed_peer, before_peer))
    finish_rows(plan, 1 - plan[0], rows, right_late, sent_ref, scratch)
    copy.wait()


def kept_kernel(
    plan,
    mixed_own,
    mixed_peer,
    before_own,
    before_peer,
    right_own,
    right_early,
    right_late,
    kept_ref,
    rights,
    scratch,
    sems,
):
    early, tile, _ = right_early.shape
    late = right_late.shape[0]
    y = plan[2]
    own = pl.ds(pl.multiple_of(y * tile, tile), tile)
    peer = pl.ds(pl.multiple_of((1 - y) * tile, tile), tile)
    copies = [
        pltpu.make_async_copy(right_own, rights.at[:, own], sems.at[0]),
        pltpu.make_async_copy(right_early, rights.at[pl.ds(0, early), peer], sems.at[1]),
        pltpu.make_async_copy(right_late, rights.at[pl.ds(early, late), peer], sems.at[2]),
    ]
    for copy in copies:
        copy.start()
    rows = ((mixed_own, before_own), (mixed_peer, before_peer))
    finish_rows(plan, plan[0], rows, right_late, kept_ref, scratch)
    for copy in copies:
        copy.wait()


def gather_pieces(plan, pieces, vector):
    x, y = plan[1], plan[2]
    _, sectors, half, _ = pieces.shape
    for xr in range(2):
        for yr in range(2):
            for sr in range(sectors):
                row = (y ^ yr) * 2 * half + (x ^ xr) * half
                at = pl.ds(pl.multiple_of(row, half), half)
                vector[plan[4] ^ sr, at, :] = pieces[2 * xr + yr, sr]


def near_kernel(sectors, plan, start, near, lefts, partial_ref, sums_ref, vector):
    terms, width, _ = lefts.shape
    half = width // 4
    core, x, y = plan[0], plan[1], plan[2]
    gather_pieces(plan, near, vector)
    cols = pl.ds(pl.multiple_of(core * width, width), width)
    inner = jnp.zeros((8, width), jnp.float32)
    norm = inner
    for k in range(terms):
        source, _ = term_of(plan, sectors, terms, k)
        partial_ref[k] = jnp.dot(lefts[k, :, cols], vector[source], preferred_element_type=jnp.float32)
        if k < 4:
            for sr in range(sectors):
                row = core * width + (y ^ (k % 2)) * 2 * half + (x ^ (k // 2)) * half
                at = pl.ds(pl.multiple_of(row, half), half)
                image = near[k, sr].astype(jnp.float32)
                before = start[plan[4] ^ sr, at, :].astype(jnp.float32)
                inner += jnp.sum((before * image).reshape(half // 8, 8, width), axis=0)
                norm += jnp.sum((image * image).reshape(half // 8, 8, width), axis=0)
    for k, value in enumerate((inner, norm)):
        sums_ref[k] = jnp.broadcast_to(jnp.sum(value), sums_ref.shape[1:])


def second_kernel(
    sectors,
    plan,
    square_ref,
    sums_ref,
    partial,
    near,
    far,
    lefts,
    rights,
    kept_ref,
    sent_ref,
    tiles_ref,
    vector,
    mixed,
    total,
):
    terms, width, _ = lefts.shape
    tile = width // 2
    half = tile // 2
    core, x, y, z = plan[0], plan[1], plan[2], plan[3]
    gather_pieces(plan, far, vector)
    cols = pl.ds(pl.multiple_of((1 - core) * width, width), width)
    for k in range(terms):
        source, weight = term_of(plan, sectors, terms, k)
        product = jnp.dot(lefts[k, :, cols], vector[source], preferred_element_type=jnp.float32)
        product = (partial[k] + product) * weight
        mixed[:, k * width : (k + 1) * width] = product.astype(jnp.bfloat16)
    total[...] = collect(mixed[...], rights)
    extra_shape = (EXTRA_ROWS, kept_ref.shape[2])
    lane = lax.broadcasted_iota(jnp.int32, extra_shape, 1)
    zeros = jnp.zeros(extra_shape, jnp.float32)
    own_sums, z_sums = zeros, zeros
    for k, value in enumerate((0.5 * square_ref[0, 0], sums_ref[0, 0, 0], sums_ref[1, 0, 0])):
        value = jnp.broadcast_to(value, extra_shape)
        own_sums = jnp.where(lane == k, value, own_sums)
        for level in range(3):
            piece = value.astype(jnp.bfloat16).astype(jnp.float32)
            z_sums = jnp.where(lane == 9 * core + 3 * k + level, piece, z_sums)
            value = value - piece

    def packed(top, bottom):
        halves = [
            jnp.concatenate([top[:, col : col + tile], bottom[:, col : col + tile]], axis=1)
            for col in (0, tile)
        ]
        return jnp.where(core == 0, halves[0], halves[1]), jnp.where(core == 0, halves[1], halves[0])

    for k, z_row in enumerate((z, 1 - z)):
        image = []
        for lower in range(2):
            piece = 2 * (x ^ lower)
            image.append(jnp.where(z_row == core, near[piece, 0], far[piece, 0]).astype(jnp.float32))
        tiles_ref[k] = packed(*image)[0].astype(tiles_ref.dtype)
    for xr in range(2):
        for zr in range(2):
            at = (
                pl.ds(pl.multiple_of((z ^ zr) * tile, tile), tile),
                pl.ds(pl.multiple_of((x ^ xr) * width, width), width),
            )
            block = total[at]
            mine, other = packed(block[:half], block[half:])
            kept_ref[2 * zr + xr, :half] = mine
            sent_ref[2 * zr + xr, :half] = other
    for to in range(4):
        kept_ref[to, half:] = (own_sums, zeros, z_sums, zeros)[to]
        sent_ref[to, half:] = (own_sums, zeros, z_sums, zeros)[to]


def last_kernel(plan, own_ref, from_x, from_z, from_xz, tiles_ref, got_ref, first_ref, out_ref):
    _, rows, cols = out_ref.shape
    half = rows // 2
    core, x, y, z, sector = plan[0], plan[1], plan[2], plan[3], plan[4]
    total = own_ref[:half] + from_x[:half].astype(jnp.float32)
    total += from_z[:half].astype(jnp.float32) + from_xz[:half].astype(jnp.float32)
    own_sums = own_ref[half : half + 8]
    z_sums = from_z[half : half + EXTRA_ROWS].astype(jnp.float32)[:8]
    image = jnp.where(x == z, tiles_ref[0], got_ref[...]).astype(jnp.float32)
    lane = lax.broadcasted_iota(jnp.int32, own_sums.shape, 1)

    def pick(values, wanted):
        return jnp.sum(jnp.where(wanted, values, 0.0), axis=1, keepdims=True)[:1]

    sums = []
    for k in range(3):
        z_part = pick(z_sums, (lane % 9 // 3 == k) & (lane < 18))
        sums.append(pick(own_sums, lane == k) + z_part)
    square, inner, norm = sums
    quotient = inner / square
    residual_square = jnp.maximum(norm - quotient * inner, 0.0)
    scale = lax.rsqrt(residual_square / square + EPSILON)
    sizes = plan[PLAN_BITS + 2 * sector], plan[PLAN_BITS + 2 * sector + 1]
    second = (total - quotient * image) * scale
    for k in range(2):
        at = slice(k * half, (k + 1) * half)
        part = slice(k * cols, (k + 1) * cols)
        first_ref[0, at] = image[:, part].astype(jnp.bfloat16)
        row = (2 * z + y) * rows + k * half
        keep = live_block(sizes, row, (2 * x + core) * cols, (half, cols))
        out_ref[0, at] = jnp.where(keep, second[:, part], 0.0).astype(jnp.bfloat16)


def on_device(
    wavefunction, left_environment, right_environment, sector_sizes, pairing, term_mask, coupling
):
    tile = wavefunction.shape[1]
    terms = left_environment.shape[0]
    sectors = lax.axis_size("sec") // SECTOR_BIT
    capacity = tile * GRID_ROWS
    bf16, f32 = jnp.bfloat16, jnp.float32

    def shaped(*shape, dtype=bf16):
        return jax.ShapeDtypeStruct(shape, dtype)

    index = lax.axis_index("sec").astype(jnp.int32)
    bits = [index % 2, index // XBIT % 2, index // YBIT % 2, index // ZBIT % 2, index // SECTOR_BIT]
    sizes = jnp.stack([sector_sizes[0], jnp.take(sector_sizes[1], pairing)], axis=1)
    group = index % GRID_COLS * terms

    def mine(table):
        row = lax.dynamic_slice(table, (bits[4], group), (1, terms))
        return row.reshape(terms)

    plan = jnp.concatenate([jnp.stack(bits), sizes.reshape(-1), mine(coupling), mine(term_mask)])

    start_tile = jnp.concatenate([wavefunction[0, : tile // 2], wavefunction[0, tile // 2 :]], axis=1)
    early = terms // 6
    tiles = [spread(start_tile, flip) for flip in range(0, lax.axis_size("sec"), SECTOR_BIT)]
    gated, tiles[0] = lax.optimization_barrier((left_environment, tiles[0]))
    tiles = jnp.stack(tiles)
    tiles = jnp.stack([tiles, exchange(tiles, YBIT)])
    right_early = exchange(right_environment[:early], YBIT)
    tiles, right_early = lax.optimization_barrier((tiles, right_early))
    tiles = jnp.stack([tiles, exchange(tiles, XBIT)])
    far_tiles = exchange(tiles, CORE)

    left_peer = exchange(gated, ZBIT)
    right_late = exchange(right_environment[early:], YBIT)

    def work(macs):
        return pl.CostEstimate(flops=int(2 * macs), bytes_accessed=terms * tile * capacity * 4, transcendentals=0)

    width = 2 * tile
    macs = terms * tile * capacity * width
    vector_shape = (sectors, capacity, width)
    unit = (4, tile // 2, width)

    def params(mib):
        return pltpu.CompilerParams(vmem_limit_bytes=mib * MIB)

    total_shape = shaped(tile, capacity, dtype=f32)
    mixed_shape = shaped(2, tile, terms * tile)
    start_vector, mixed_own, total_own, square, left_own, right_own = pl.pallas_call(
        lambda *refs: start_kernel(sectors, *refs),
        out_shape=[
            shaped(*vector_shape),
            mixed_shape,
            total_shape,
            shaped(8, 128, dtype=f32),
            shaped(terms, tile, capacity),
            shaped(terms, tile, capacity),
        ],
        in_specs=[smem(), vmem(), vmem(), anywhere(), anywhere(), vmem()],
        out_specs=[vmem()] * 6,
        scratch_shapes=[pltpu.SemaphoreType.DMA((2,))],
        compiler_params=params(16),
        cost_estimate=work(START_COST * macs),
    )(plan, tiles, far_tiles, left_environment, right_environment, right_early)
    mixed_peer, total_peer, lefts = pl.pallas_call(
        lambda *refs: peer_kernel(sectors, *refs),
        out_shape=[mixed_shape, total_shape, shaped(terms, width, capacity)],
        in_specs=[smem()] + [vmem()] * 5,
        out_specs=[vmem()] * 3,
        scratch_shapes=[pltpu.SemaphoreType.DMA((2,))],
        compiler_params=params(PEER_MIB),
        cost_estimate=work(PEER_COST * macs),
    )(plan, start_vector, left_own, left_peer, right_own, right_early)
    late_shape = shaped(terms - early, tile, capacity)
    sent, right_late = pl.pallas_call(
        sent_kernel,
        out_shape=[shaped(*unit, dtype=f32), late_shape],
        in_specs=[smem()] + [vmem()] * 5,
        out_specs=[vmem()] * 2,
        scratch_shapes=[pltpu.VMEM((tile, capacity), f32), pltpu.SemaphoreType.DMA],
        compiler_params=params(16),
        cost_estimate=work(macs),
    )(plan, mixed_own, mixed_peer, total_own, total_peer, right_late)
    kept, rights = pl.pallas_call(
        kept_kernel,
        out_shape=[shaped(*unit, dtype=f32), shaped(terms, width, capacity)],
        in_specs=[smem()] + [vmem()] * 7,
        out_specs=[vmem()] * 2,
        scratch_shapes=[pltpu.VMEM((tile, capacity), f32), pltpu.SemaphoreType.DMA((3,))],
        compiler_params=params(16),
        cost_estimate=work(macs),
    )(plan, mixed_own, mixed_peer, total_own, total_peer, right_own, right_early, right_late)

    summed = kept + exchange(sent, CORE)
    image_unit = (
        summed[0]
        + exchange(summed[1].astype(bf16), XBIT).astype(f32)
        + exchange(summed[2].astype(bf16), ZBIT).astype(f32)
        + exchange(summed[3].astype(bf16), XBIT | ZBIT).astype(f32)
    )
    units = image_unit.astype(bf16)[None]
    flip = SECTOR_BIT
    while flip < lax.axis_size("sec"):
        units = jnp.concatenate([units, exchange(units, flip)])
        flip *= 2
    units = jnp.stack(
        [units, exchange(units, YBIT), exchange(units, XBIT), exchange(units, XBIT | YBIT)]
    )
    far_units = exchange(units, CORE)
    half = tile // 2
    part = (4, half + EXTRA_ROWS, width)
    near_shape = (sectors, width, width)
    partial, sums = pl.pallas_call(
        lambda *refs: near_kernel(sectors, *refs),
        out_shape=[shaped(terms, width, width, dtype=f32), shaped(2, 8, 128, dtype=f32)],
        in_specs=[smem()] + [vmem()] * 3,
        out_specs=[vmem()] * 2,
        scratch_shapes=[pltpu.VMEM(near_shape, bf16)],
        compiler_params=params(20),
        cost_estimate=work(macs),
    )(plan, start_vector, units, lefts)
    kept, sent, image_tiles = pl.pallas_call(
        lambda *refs: second_kernel(sectors, *refs),
        out_shape=[shaped(*part, dtype=f32)] * 2 + [shaped(2, half, width)],
        in_specs=[smem()] + [vmem()] * 7,
        out_specs=[vmem()] * 3,
        scratch_shapes=[
            pltpu.VMEM(near_shape, bf16),
            pltpu.VMEM((width, terms * width), bf16),
            pltpu.VMEM((width, capacity), f32),
        ],
        compiler_params=params(24),
        cost_estimate=work(3 * macs),
    )(plan, square, sums, partial, units, far_units, lefts, rights)
    got_tile = exchange(image_tiles[1], ZBIT)
    summed = kept + exchange(sent, CORE)
    first, second = pl.pallas_call(
        last_kernel,
        out_shape=[shaped(1, tile, tile)] * 2,
        in_specs=[smem()] + [vmem()] * 6,
        out_specs=[vmem()] * 2,
        compiler_params=params(4),
    )(
        plan,
        summed[0],
        exchange(summed[1].astype(bf16), XBIT),
        exchange(summed[2].astype(bf16), ZBIT),
        exchange(summed[3].astype(bf16), XBIT | ZBIT),
        image_tiles,
        got_tile,
    )
    return first, second


def solution(mesh):
    return jax.shard_map(
        on_device,
        mesh=mesh,
        in_specs=(
            P(("groups", "sec"), None, None),
            P(("groups", "sec"), None, None),
            P(("groups", "sec"), None, None),
            P(None, "groups"),
            P("groups"),
            P("groups", None),
            P("groups", None),
        ),
        out_specs=(P(("groups", "sec"), None, None), P(("groups", "sec"), None, None)),
        check_vma=False,
    )
```

```python
import jax
import jax.numpy as jnp
from jax import lax
from jax.experimental import pallas as pl
from jax.experimental.pallas import tpu as pltpu
from jax.sharding import PartitionSpec as P

GRID_ROWS = 4
GRID_COLS = 4
CORE, XBIT, YBIT, ZBIT = 1, 2, 4, 8
SECTOR_BIT = GRID_ROWS * GRID_COLS
EPSILON = 1e-06
EXTRA_ROWS = 16
MIB = 2**20
START_COST = 3
PEER_COST = 1
PEER_MIB = 16
PLAN_BITS = 5


def exchange(block, flip):
    return lax.ppermute(block, "sec", [(i, i ^ flip) for i in range(lax.axis_size("sec"))])


def spread(tile, flip):
    route = []
    for i in range(lax.axis_size("sec")):
        x, z = i // XBIT % 2, i // ZBIT % 2
        new_x = x ^ z if flip >= SECTOR_BIT else z
        route.append((i, i + (new_x - x) * XBIT + (x - z) * ZBIT ^ flip))
    return lax.ppermute(tile, "sec", route)


def smem():
    return pl.BlockSpec(memory_space=pltpu.SMEM)


def vmem():
    return pl.BlockSpec(memory_space=pltpu.VMEM)


def anywhere():
    return pl.BlockSpec(memory_space=pl.ANY)


def live_block(sizes, row_start, col_start, shape):
    rows = row_start + lax.broadcasted_iota(jnp.int32, shape, 0)
    cols = col_start + lax.broadcasted_iota(jnp.int32, shape, 1)
    return (rows < sizes[0]) & (cols < sizes[1])


def term_of(plan, sectors, terms, k):
    base = PLAN_BITS + 2 * sectors
    return plan[base + k], plan[base + terms + k].astype(jnp.float32)


def mix(plan, sectors, terms, k, left, vector):
    source, weight = term_of(plan, sectors, terms, k)
    return jnp.dot(left, vector[source], preferred_element_type=jnp.float32) * weight


def put_pair(mixed, k, pair):
    tile = pair[0].shape[1] // 2
    for half in range(2):
        at = slice(half * tile, (half + 1) * tile)
        both = jnp.concatenate([product[:, at] for product in pair], axis=1)
        mixed[half, :, k * tile : (k + 2) * tile] = both.astype(jnp.bfloat16)


def collect(mixed, rights):
    terms, tile, width = rights.shape
    flat = rights[...].reshape(terms * tile, width)
    return jnp.dot(mixed, flat, preferred_element_type=jnp.float32)


def start_kernel(
    sectors,
    plan,
    near,
    far,
    left_own,
    right_own,
    right_early,
    vector,
    mixed_ref,
    total_ref,
    square_ref,
    lefts,
    rights,
    sems,
):
    terms, tile, _ = left_own.shape
    early = right_early.shape[0] * tile
    width = 2 * tile
    core, x, y, z = plan[0], plan[1], plan[2], plan[3]
    copies = [
        pltpu.make_async_copy(left_own, lefts, sems.at[0]),
        pltpu.make_async_copy(right_own, rights, sems.at[1]),
    ]
    for copy in copies:
        copy.start()
    square = jnp.zeros((8, width), jnp.float32)
    for xr in range(2):
        for yr in range(2):
            for sr in range(sectors):
                sector = plan[4] ^ sr
                z_row = x ^ xr ^ z if sr else x ^ xr
                row = (2 * z_row + (y ^ yr)) * tile
                sizes = plan[PLAN_BITS + 2 * sector], plan[PLAN_BITS + 2 * sector + 1]
                mine, other = near[xr, yr, sr], far[xr, yr, sr]
                low = jnp.where(core == 0, mine, other).astype(jnp.float32)
                high = jnp.where(core == 0, other, mine).astype(jnp.float32)
                top = jnp.concatenate([low[:, :tile], high[:, :tile]], axis=1)
                bottom = jnp.concatenate([low[:, tile:], high[:, tile:]], axis=1)
                both = jnp.concatenate([top, bottom], axis=0)
                both = jnp.where(live_block(sizes, row, z * width, both.shape), both, 0.0)
                square += jnp.sum((both * both).reshape(tile // 8, 8, width), axis=0)
                at = pl.ds(pl.multiple_of(row, tile), tile)
                vector[sector, at, :] = both.astype(jnp.bfloat16)
    square_ref[...] = jnp.broadcast_to(jnp.sum(square), square_ref.shape)
    copies[0].wait()
    for k in range(0, terms, 2):
        pair = [mix(plan, sectors, terms, i, lefts[i], vector) for i in (k, k + 1)]
        put_pair(mixed_ref, k, pair)
    copies[1].wait()
    total = collect(mixed_ref[y], rights)
    total_ref[...] = total + collect(mixed_ref[1 - y][:, :early], right_early)


def peer_kernel(
    sectors,
    plan,
    vector,
    left_own,
    left_peer,
    right_own,
    right_early,
    mixed,
    total_ref,
    lefts,
    sems,
):
    terms, tile, _ = left_peer.shape
    early = right_early.shape[0] * tile
    y, z = plan[2], plan[3]
    own = pl.ds(pl.multiple_of(z * tile, tile), tile)
    peer = pl.ds(pl.multiple_of((1 - z) * tile, tile), tile)
    copies = [
        pltpu.make_async_copy(left_own, lefts.at[:, own], sems.at[0]),
        pltpu.make_async_copy(left_peer, lefts.at[:, peer], sems.at[1]),
    ]
    for copy in copies:
        copy.start()
    for k in range(0, terms, 2):
        pair = [mix(plan, sectors, terms, i, left_peer[i], vector) for i in (k, k + 1)]
        put_pair(mixed, k, pair)
    total_ref[...] = collect(mixed[y], right_own) + collect(mixed[1 - y][:, :early], right_early)
    for copy in copies:
        copy.wait()


def finish_rows(plan, mine, rows, right_late, unit_ref, scratch):
    late, tile, _ = right_late.shape
    x, y, z = plan[1], plan[2], plan[3]
    (mixed_own, before_own), (mixed_peer, before_peer) = rows
    is_own = mine == z
    first = mixed_own.shape[2] - late * tile
    mixed = jnp.where(is_own, mixed_own[1 - y], mixed_peer[1 - y])[:, first:]
    total = jnp.where(is_own, before_own[...], before_peer[...]) + collect(mixed, right_late)
    sizes = plan[PLAN_BITS + 2 * plan[4]], plan[PLAN_BITS + 2 * plan[4] + 1]
    keep = live_block(sizes, (2 * mine + y) * tile, 0, total.shape)
    scratch[...] = jnp.where(keep, total, 0.0)
    _, unit_rows, unit_cols = unit_ref.shape
    for xr in range(2):
        for zr in range(2):
            at = (
                pl.ds(pl.multiple_of((x ^ xr) * unit_rows, unit_rows), unit_rows),
                pl.ds(pl.multiple_of((z ^ zr) * unit_cols, unit_cols), unit_cols),
            )
            unit_ref[2 * zr + xr] = scratch[at]


def sent_kernel(
    plan, mixed_own, mixed_peer, before_own, before_peer, right_late, sent_ref, late_ref, scratch, sem
):
    copy = pltpu.make_async_copy(right_late, late_ref, sem)
    copy.start()
    rows = ((mixed_own, before_own), (mixed_peer, before_peer))
    finish_rows(plan, 1 - plan[0], rows, right_late, sent_ref, scratch)
    copy.wait()


def kept_kernel(
    plan,
    mixed_own,
    mixed_peer,
    before_own,
    before_peer,
    right_own,
    right_early,
    right_late,
    kept_ref,
    rights,
    scratch,
    sems,
):
    early, tile, _ = right_early.shape
    late = right_late.shape[0]
    y = plan[2]
    own = pl.ds(pl.multiple_of(y * tile, tile), tile)
    peer = pl.ds(pl.multiple_of((1 - y) * tile, tile), tile)
    copies = [
        pltpu.make_async_copy(right_own, rights.at[:, own], sems.at[0]),
        pltpu.make_async_copy(right_early, rights.at[pl.ds(0, early), peer], sems.at[1]),
        pltpu.make_async_copy(right_late, rights.at[pl.ds(early, late), peer], sems.at[2]),
    ]
    for copy in copies:
        copy.start()
    rows = ((mixed_own, before_own), (mixed_peer, before_peer))
    finish_rows(plan, plan[0], rows, right_late, kept_ref, scratch)
    for copy in copies:
        copy.wait()


def gather_pieces(plan, pieces, vector):
    x, y = plan[1], plan[2]
    _, sectors, half, _ = pieces.shape
    for xr in range(2):
        for yr in range(2):
            for sr in range(sectors):
                row = (y ^ yr) * 2 * half + (x ^ xr) * half
                at = pl.ds(pl.multiple_of(row, half), half)
                vector[plan[4] ^ sr, at, :] = pieces[2 * xr + yr, sr]


def near_kernel(sectors, plan, start, near, lefts, partial_ref, sums_ref, vector):
    terms, width, _ = lefts.shape
    half = width // 4
    core, x, y = plan[0], plan[1], plan[2]
    gather_pieces(plan, near, vector)
    cols = pl.ds(pl.multiple_of(core * width, width), width)
    inner = jnp.zeros((8, width), jnp.float32)
    norm = inner
    for k in range(terms):
        source, _ = term_of(plan, sectors, terms, k)
        partial_ref[k] = jnp.dot(lefts[k, :, cols], vector[source], preferred_element_type=jnp.float32)
        if k < 4:
            for sr in range(sectors):
                row = core * width + (y ^ (k % 2)) * 2 * half + (x ^ (k // 2)) * half
                at = pl.ds(pl.multiple_of(row, half), half)
                image = near[k, sr].astype(jnp.float32)
                before = start[plan[4] ^ sr, at, :].astype(jnp.float32)
                inner += jnp.sum((before * image).reshape(half // 8, 8, width), axis=0)
                norm += jnp.sum((image * image).reshape(half // 8, 8, width), axis=0)
    for k, value in enumerate((inner, norm)):
        sums_ref[k] = jnp.broadcast_to(jnp.sum(value), sums_ref.shape[1:])


def second_kernel(
    sectors,
    plan,
    square_ref,
    sums_ref,
    partial,
    near,
    far,
    lefts,
    rights,
    kept_ref,
    sent_ref,
    tiles_ref,
    vector,
    mixed,
    total,
):
    terms, width, _ = lefts.shape
    tile = width // 2
    half = tile // 2
    core, x, y, z = plan[0], plan[1], plan[2], plan[3]
    gather_pieces(plan, far, vector)
    cols = pl.ds(pl.multiple_of((1 - core) * width, width), width)
    for k in range(terms):
        source, weight = term_of(plan, sectors, terms, k)
        product = jnp.dot(lefts[k, :, cols], vector[source], preferred_element_type=jnp.float32)
        product = (partial[k] + product) * weight
        mixed[:, k * width : (k + 1) * width] = product.astype(jnp.bfloat16)
    total[...] = collect(mixed[...], rights)
    extra_shape = (EXTRA_ROWS, kept_ref.shape[2])
    lane = lax.broadcasted_iota(jnp.int32, extra_shape, 1)
    zeros = jnp.zeros(extra_shape, jnp.float32)
    own_sums, z_sums = zeros, zeros
    for k, value in enumerate((0.5 * square_ref[0, 0], sums_ref[0, 0, 0], sums_ref[1, 0, 0])):
        value = jnp.broadcast_to(value, extra_shape)
        own_sums = jnp.where(lane == k, value, own_sums)
        for level in range(3):
            piece = value.astype(jnp.bfloat16).astype(jnp.float32)
            z_sums = jnp.where(lane == 9 * core + 3 * k + level, piece, z_sums)
            value = value - piece

    def packed(top, bottom):
        halves = [
            jnp.concatenate([top[:, col : col + tile], bottom[:, col : col + tile]], axis=1)
            for col in (0, tile)
        ]
        return jnp.where(core == 0, halves[0], halves[1]), jnp.where(core == 0, halves[1], halves[0])

    for k, z_row in enumerate((z, 1 - z)):
        image = []
        for lower in range(2):
            piece = 2 * (x ^ lower)
            image.append(jnp.where(z_row == core, near[piece, 0], far[piece, 0]).astype(jnp.float32))
        tiles_ref[k] = packed(*image)[0].astype(tiles_ref.dtype)
    for xr in range(2):
        for zr in range(2):
            at = (
                pl.ds(pl.multiple_of((z ^ zr) * tile, tile), tile),
                pl.ds(pl.multiple_of((x ^ xr) * width, width), width),
            )
            block = total[at]
            mine, other = packed(block[:half], block[half:])
            kept_ref[2 * zr + xr, :half] = mine
            sent_ref[2 * zr + xr, :half] = other
    for to in range(4):
        kept_ref[to, half:] = (own_sums, zeros, z_sums, zeros)[to]
        sent_ref[to, half:] = (own_sums, zeros, z_sums, zeros)[to]


def last_kernel(plan, own_ref, from_x, from_z, from_xz, tiles_ref, got_ref, first_ref, out_ref):
    _, rows, cols = out_ref.shape
    half = rows // 2
    core, x, y, z, sector = plan[0], plan[1], plan[2], plan[3], plan[4]
    total = own_ref[:half] + from_x[:half].astype(jnp.float32)
    total += from_z[:half].astype(jnp.float32) + from_xz[:half].astype(jnp.float32)
    own_sums = own_ref[half : half + 8]
    z_sums = from_z[half : half + EXTRA_ROWS].astype(jnp.float32)[:8]
    image = jnp.where(x == z, tiles_ref[0], got_ref[...]).astype(jnp.float32)
    lane = lax.broadcasted_iota(jnp.int32, own_sums.shape, 1)

    def pick(values, wanted):
        return jnp.sum(jnp.where(wanted, values, 0.0), axis=1, keepdims=True)[:1]

    sums = []
    for k in range(3):
        z_part = pick(z_sums, (lane % 9 // 3 == k) & (lane < 18))
        sums.append(pick(own_sums, lane == k) + z_part)
    square, inner, norm = sums
    quotient = inner / square
    residual_square = jnp.maximum(norm - quotient * inner, 0.0)
    scale = lax.rsqrt(residual_square / square + EPSILON)
    sizes = plan[PLAN_BITS + 2 * sector], plan[PLAN_BITS + 2 * sector + 1]
    second = (total - quotient * image) * scale
    for k in range(2):
        at = slice(k * half, (k + 1) * half)
        part = slice(k * cols, (k + 1) * cols)
        first_ref[0, at] = image[:, part].astype(jnp.bfloat16)
        row = (2 * z + y) * rows + k * half
        keep = live_block(sizes, row, (2 * x + core) * cols, (half, cols))
        out_ref[0, at] = jnp.where(keep, second[:, part], 0.0).astype(jnp.bfloat16)


def on_device(
    wavefunction, left_environment, right_environment, sector_sizes, pairing, term_mask, coupling
):
    tile = wavefunction.shape[1]
    terms = left_environment.shape[0]
    sectors = lax.axis_size("sec") // SECTOR_BIT
    capacity = tile * GRID_ROWS
    bf16, f32 = jnp.bfloat16, jnp.float32

    def shaped(*shape, dtype=bf16):
        return jax.ShapeDtypeStruct(shape, dtype)

    index = lax.axis_index("sec").astype(jnp.int32)
    bits = [index % 2, index // XBIT % 2, index // YBIT % 2, index // ZBIT % 2, index // SECTOR_BIT]
    sizes = jnp.stack([sector_sizes[0], jnp.take(sector_sizes[1], pairing)], axis=1)
    group = index % GRID_COLS * terms

    def mine(table):
        row = lax.dynamic_slice(table, (bits[4], group), (1, terms))
        return row.reshape(terms)

    plan = jnp.concatenate([jnp.stack(bits), sizes.reshape(-1), mine(coupling), mine(term_mask)])

    start_tile = jnp.concatenate([wavefunction[0, : tile // 2], wavefunction[0, tile // 2 :]], axis=1)
    early = terms // 6
    tiles = [spread(start_tile, flip) for flip in range(0, lax.axis_size("sec"), SECTOR_BIT)]
    gated, tiles[0] = lax.optimization_barrier((left_environment, tiles[0]))
    tiles = jnp.stack(tiles)
    tiles = jnp.stack([tiles, exchange(tiles, YBIT)])
    right_early = exchange(right_environment[:early], YBIT)
    tiles, right_early = lax.optimization_barrier((tiles, right_early))
    tiles = jnp.stack([tiles, exchange(tiles, XBIT)])
    far_tiles = exchange(tiles, CORE)

    left_peer = exchange(gated, ZBIT)
    right_late = exchange(right_environment[early:], YBIT)

    def work(macs):
        return pl.CostEstimate(flops=int(2 * macs), bytes_accessed=terms * tile * capacity * 4, transcendentals=0)

    width = 2 * tile
    macs = terms * tile * capacity * width
    vector_shape = (sectors, capacity, width)
    unit = (4, tile // 2, width)

    def params(mib):
        return pltpu.CompilerParams(vmem_limit_bytes=mib * MIB)

    total_shape = shaped(tile, capacity, dtype=f32)
    mixed_shape = shaped(2, tile, terms * tile)
    start_vector, mixed_own, total_own, square, left_own, right_own = pl.pallas_call(
        lambda *refs: start_kernel(sectors, *refs),
        out_shape=[
            shaped(*vector_shape),
            mixed_shape,
            total_shape,
            shaped(8, 128, dtype=f32),
            shaped(terms, tile, capacity),
            shaped(terms, tile, capacity),
        ],
        in_specs=[smem(), vmem(), vmem(), anywhere(), anywhere(), vmem()],
        out_specs=[vmem()] * 6,
        scratch_shapes=[pltpu.SemaphoreType.DMA((2,))],
        compiler_params=params(16),
        cost_estimate=work(START_COST * macs),
    )(plan, tiles, far_tiles, left_environment, right_environment, right_early)
    mixed_peer, total_peer, lefts = pl.pallas_call(
        lambda *refs: peer_kernel(sectors, *refs),
        out_shape=[mixed_shape, total_shape, shaped(terms, width, capacity)],
        in_specs=[smem()] + [vmem()] * 5,
        out_specs=[vmem()] * 3,
        scratch_shapes=[pltpu.SemaphoreType.DMA((2,))],
        compiler_params=params(PEER_MIB),
        cost_estimate=work(PEER_COST * macs),
    )(plan, start_vector, left_own, left_peer, right_own, right_early)
    late_shape = shaped(terms - early, tile, capacity)
    sent, right_late = pl.pallas_call(
        sent_kernel,
        out_shape=[shaped(*unit, dtype=f32), late_shape],
        in_specs=[smem()] + [vmem()] * 5,
        out_specs=[vmem()] * 2,
        scratch_shapes=[pltpu.VMEM((tile, capacity), f32), pltpu.SemaphoreType.DMA],
        compiler_params=params(16),
        cost_estimate=work(macs),
    )(plan, mixed_own, mixed_peer, total_own, total_peer, right_late)
    kept, rights = pl.pallas_call(
        kept_kernel,
        out_shape=[shaped(*unit, dtype=f32), shaped(terms, width, capacity)],
        in_specs=[smem()] + [vmem()] * 7,
        out_specs=[vmem()] * 2,
        scratch_shapes=[pltpu.VMEM((tile, capacity), f32), pltpu.SemaphoreType.DMA((3,))],
        compiler_params=params(16),
        cost_estimate=work(macs),
    )(plan, mixed_own, mixed_peer, total_own, total_peer, right_own, right_early, right_late)

    summed = kept + exchange(sent, CORE)
    image_unit = (
        summed[0]
        + exchange(summed[1].astype(bf16), XBIT).astype(f32)
        + exchange(summed[2].astype(bf16), ZBIT).astype(f32)
        + exchange(summed[3].astype(bf16), XBIT | ZBIT).astype(f32)
    )
    own_unit = image_unit.astype(bf16)[None]
    gathered = own_unit
    flip = SECTOR_BIT
    while flip < lax.axis_size("sec"):
        gathered = jnp.concatenate([gathered, exchange(gathered, flip)])
        flip *= 2
    units = [gathered]
    for way in (YBIT, XBIT, XBIT | YBIT):
        parts = [exchange(own_unit, way)]
        if sectors > 1:
            parts.append(exchange(gathered[1:], way))
        units.append(jnp.concatenate(parts))
    units = jnp.stack(units)
    far_units = exchange(units, CORE)
    half = tile // 2
    part = (4, half + EXTRA_ROWS, width)
    near_shape = (sectors, width, width)
    partial, sums = pl.pallas_call(
        lambda *refs: near_kernel(sectors, *refs),
        out_shape=[shaped(terms, width, width, dtype=f32), shaped(2, 8, 128, dtype=f32)],
        in_specs=[smem()] + [vmem()] * 3,
        out_specs=[vmem()] * 2,
        scratch_shapes=[pltpu.VMEM(near_shape, bf16)],
        compiler_params=params(20),
        cost_estimate=work(macs),
    )(plan, start_vector, units, lefts)
    kept, sent, image_tiles = pl.pallas_call(
        lambda *refs: second_kernel(sectors, *refs),
        out_shape=[shaped(*part, dtype=f32)] * 2 + [shaped(2, half, width)],
        in_specs=[smem()] + [vmem()] * 7,
        out_specs=[vmem()] * 3,
        scratch_shapes=[
            pltpu.VMEM(near_shape, bf16),
            pltpu.VMEM((width, terms * width), bf16),
            pltpu.VMEM((width, capacity), f32),
        ],
        compiler_params=params(24),
        cost_estimate=work(3 * macs),
    )(plan, square, sums, partial, units, far_units, lefts, rights)
    got_tile = exchange(image_tiles[1], ZBIT)
    summed = kept + exchange(sent, CORE)
    first, second = pl.pallas_call(
        last_kernel,
        out_shape=[shaped(1, tile, tile)] * 2,
        in_specs=[smem()] + [vmem()] * 6,
        out_specs=[vmem()] * 2,
        compiler_params=params(4),
    )(
        plan,
        summed[0],
        exchange(summed[1].astype(bf16), XBIT),
        exchange(summed[2].astype(bf16), ZBIT),
        exchange(summed[3].astype(bf16), XBIT | ZBIT),
        image_tiles,
        got_tile,
    )
    return first, second


def solution(mesh):
    return jax.shard_map(
        on_device,
        mesh=mesh,
        in_specs=(
            P(("groups", "sec"), None, None),
            P(("groups", "sec"), None, None),
            P(("groups", "sec"), None, None),
            P(None, "groups"),
            P("groups"),
            P("groups", None),
            P("groups", None),
        ),
        out_specs=(P(("groups", "sec"), None, None), P(("groups", "sec"), None, None)),
        check_vma=False,
    )
```

```python
import jax
import jax.numpy as jnp
from jax import lax
from jax.experimental import pallas as pl
from jax.experimental.pallas import tpu as pltpu
from jax.sharding import PartitionSpec as P

GRID_ROWS = 4
GRID_COLS = 4
CORE, XBIT, YBIT, ZBIT = 1, 2, 4, 8
SECTOR_BIT = GRID_ROWS * GRID_COLS
EPSILON = 1e-06
EXTRA_ROWS = 16
MIB = 2**20
START_COST = 3
PEER_COST = 1
PEER_MIB = 16
PLAN_BITS = 5


def exchange(block, flip):
    return lax.ppermute(block, "sec", [(i, i ^ flip) for i in range(lax.axis_size("sec"))])


def spread(tile, flip):
    route = []
    for i in range(lax.axis_size("sec")):
        x, z = i // XBIT % 2, i // ZBIT % 2
        new_x = x ^ z if flip >= SECTOR_BIT else z
        route.append((i, i + (new_x - x) * XBIT + (x - z) * ZBIT ^ flip))
    return lax.ppermute(tile, "sec", route)


def smem():
    return pl.BlockSpec(memory_space=pltpu.SMEM)


def vmem():
    return pl.BlockSpec(memory_space=pltpu.VMEM)


def anywhere():
    return pl.BlockSpec(memory_space=pl.ANY)


def live_block(sizes, row_start, col_start, shape):
    rows = row_start + lax.broadcasted_iota(jnp.int32, shape, 0)
    cols = col_start + lax.broadcasted_iota(jnp.int32, shape, 1)
    return (rows < sizes[0]) & (cols < sizes[1])


def term_of(plan, sectors, terms, k):
    base = PLAN_BITS + 2 * sectors
    return plan[base + k], plan[base + terms + k].astype(jnp.float32)


def mix(plan, sectors, terms, k, left, vector):
    source, weight = term_of(plan, sectors, terms, k)
    return jnp.dot(left, vector[source], preferred_element_type=jnp.float32) * weight


def put_pair(mixed, k, pair):
    tile = pair[0].shape[1] // 2
    for half in range(2):
        at = slice(half * tile, (half + 1) * tile)
        both = jnp.concatenate([product[:, at] for product in pair], axis=1)
        mixed[half, :, k * tile : (k + 2) * tile] = both.astype(jnp.bfloat16)


def collect(mixed, rights):
    terms, tile, width = rights.shape
    flat = rights[...].reshape(terms * tile, width)
    return jnp.dot(mixed, flat, preferred_element_type=jnp.float32)


def start_kernel(
    sectors,
    plan,
    near,
    far,
    left_own,
    right_own,
    right_early,
    vector,
    mixed_ref,
    total_ref,
    square_ref,
    lefts,
    rights,
    sems,
):
    terms, tile, _ = left_own.shape
    early = right_early.shape[0] * tile
    width = 2 * tile
    core, x, y, z = plan[0], plan[1], plan[2], plan[3]
    copies = [
        pltpu.make_async_copy(left_own, lefts, sems.at[0]),
        pltpu.make_async_copy(right_own, rights, sems.at[1]),
    ]
    for copy in copies:
        copy.start()
    square = jnp.zeros((8, width), jnp.float32)
    for xr in range(2):
        for yr in range(2):
            for sr in range(sectors):
                sector = plan[4] ^ sr
                z_row = x ^ xr ^ z if sr else x ^ xr
                row = (2 * z_row + (y ^ yr)) * tile
                sizes = plan[PLAN_BITS + 2 * sector], plan[PLAN_BITS + 2 * sector + 1]
                mine, other = near[xr, yr, sr], far[xr, yr, sr]
                low = jnp.where(core == 0, mine, other).astype(jnp.float32)
                high = jnp.where(core == 0, other, mine).astype(jnp.float32)
                top = jnp.concatenate([low[:, :tile], high[:, :tile]], axis=1)
                bottom = jnp.concatenate([low[:, tile:], high[:, tile:]], axis=1)
                both = jnp.concatenate([top, bottom], axis=0)
                both = jnp.where(live_block(sizes, row, z * width, both.shape), both, 0.0)
                square += jnp.sum((both * both).reshape(tile // 8, 8, width), axis=0)
                at = pl.ds(pl.multiple_of(row, tile), tile)
                vector[sector, at, :] = both.astype(jnp.bfloat16)
    square_ref[...] = jnp.broadcast_to(jnp.sum(square), square_ref.shape)
    copies[0].wait()
    for k in range(0, terms, 2):
        pair = [mix(plan, sectors, terms, i, lefts[i], vector) for i in (k, k + 1)]
        put_pair(mixed_ref, k, pair)
    copies[1].wait()
    total = collect(mixed_ref[y], rights)
    total_ref[...] = total + collect(mixed_ref[1 - y][:, :early], right_early)


def peer_kernel(
    sectors,
    plan,
    vector,
    left_own,
    left_peer,
    right_own,
    right_early,
    mixed,
    total_ref,
    lefts,
    sems,
):
    terms, tile, _ = left_peer.shape
    early = right_early.shape[0] * tile
    y, z = plan[2], plan[3]
    own = pl.ds(pl.multiple_of(z * tile, tile), tile)
    peer = pl.ds(pl.multiple_of((1 - z) * tile, tile), tile)
    copies = [
        pltpu.make_async_copy(left_own, lefts.at[:, own], sems.at[0]),
        pltpu.make_async_copy(left_peer, lefts.at[:, peer], sems.at[1]),
    ]
    for copy in copies:
        copy.start()
    for k in range(0, terms, 2):
        pair = [mix(plan, sectors, terms, i, left_peer[i], vector) for i in (k, k + 1)]
        put_pair(mixed, k, pair)
    total_ref[...] = collect(mixed[y], right_own) + collect(mixed[1 - y][:, :early], right_early)
    for copy in copies:
        copy.wait()


def finish_rows(plan, mine, rows, right_late, unit_ref, scratch):
    late, tile, _ = right_late.shape
    x, y, z = plan[1], plan[2], plan[3]
    (mixed_own, before_own), (mixed_peer, before_peer) = rows
    is_own = mine == z
    first = mixed_own.shape[2] - late * tile
    mixed = jnp.where(is_own, mixed_own[1 - y], mixed_peer[1 - y])[:, first:]
    total = jnp.where(is_own, before_own[...], before_peer[...]) + collect(mixed, right_late)
    sizes = plan[PLAN_BITS + 2 * plan[4]], plan[PLAN_BITS + 2 * plan[4] + 1]
    keep = live_block(sizes, (2 * mine + y) * tile, 0, total.shape)
    scratch[...] = jnp.where(keep, total, 0.0)
    _, unit_rows, unit_cols = unit_ref.shape
    for xr in range(2):
        for zr in range(2):
            at = (
                pl.ds(pl.multiple_of((x ^ xr) * unit_rows, unit_rows), unit_rows),
                pl.ds(pl.multiple_of((z ^ zr) * unit_cols, unit_cols), unit_cols),
            )
            unit_ref[2 * zr + xr] = scratch[at]


def sent_kernel(
    plan, mixed_own, mixed_peer, before_own, before_peer, right_late, sent_ref, late_ref, scratch, sem
):
    copy = pltpu.make_async_copy(right_late, late_ref, sem)
    copy.start()
    rows = ((mixed_own, before_own), (mixed_peer, before_peer))
    finish_rows(plan, 1 - plan[0], rows, right_late, sent_ref, scratch)
    copy.wait()


def kept_kernel(
    plan,
    mixed_own,
    mixed_peer,
    before_own,
    before_peer,
    right_own,
    right_early,
    right_late,
    kept_ref,
    rights,
    scratch,
    sems,
):
    early, tile, _ = right_early.shape
    late = right_late.shape[0]
    y = plan[2]
    own = pl.ds(pl.multiple_of(y * tile, tile), tile)
    peer = pl.ds(pl.multiple_of((1 - y) * tile, tile), tile)
    copies = [
        pltpu.make_async_copy(right_own, rights.at[:, own], sems.at[0]),
        pltpu.make_async_copy(right_early, rights.at[pl.ds(0, early), peer], sems.at[1]),
        pltpu.make_async_copy(right_late, rights.at[pl.ds(early, late), peer], sems.at[2]),
    ]
    for copy in copies:
        copy.start()
    rows = ((mixed_own, before_own), (mixed_peer, before_peer))
    finish_rows(plan, plan[0], rows, right_late, kept_ref, scratch)
    for copy in copies:
        copy.wait()


def gather_pieces(plan, pieces, vector):
    x, y = plan[1], plan[2]
    _, sectors, half, _ = pieces.shape
    for xr in range(2):
        for yr in range(2):
            for sr in range(sectors):
                row = (y ^ yr) * 2 * half + (x ^ xr) * half
                at = pl.ds(pl.multiple_of(row, half), half)
                vector[plan[4] ^ sr, at, :] = pieces[2 * xr + yr, sr]


def near_kernel(sectors, plan, start, near, lefts, partial_ref, sums_ref, vector):
    terms, width, _ = lefts.shape
    half = width // 4
    core, x, y = plan[0], plan[1], plan[2]
    gather_pieces(plan, near, vector)
    cols = pl.ds(pl.multiple_of(core * width, width), width)
    inner = jnp.zeros((8, width), jnp.float32)
    norm = inner
    for k in range(terms):
        source, _ = term_of(plan, sectors, terms, k)
        partial_ref[k] = jnp.dot(lefts[k, :, cols], vector[source], preferred_element_type=jnp.float32)
        if k < 4:
            for sr in range(sectors):
                row = core * width + (y ^ (k % 2)) * 2 * half + (x ^ (k // 2)) * half
                at = pl.ds(pl.multiple_of(row, half), half)
                image = near[k, sr].astype(jnp.float32)
                before = start[plan[4] ^ sr, at, :].astype(jnp.float32)
                inner += jnp.sum((before * image).reshape(half // 8, 8, width), axis=0)
                norm += jnp.sum((image * image).reshape(half // 8, 8, width), axis=0)
    for k, value in enumerate((inner, norm)):
        sums_ref[k] = jnp.broadcast_to(jnp.sum(value), sums_ref.shape[1:])


def second_kernel(
    sectors,
    plan,
    square_ref,
    sums_ref,
    partial,
    near,
    far,
    lefts,
    rights,
    kept_ref,
    sent_ref,
    tiles_ref,
    vector,
    mixed,
    total,
):
    terms, width, _ = lefts.shape
    tile = width // 2
    half = tile // 2
    core, x, y, z = plan[0], plan[1], plan[2], plan[3]
    gather_pieces(plan, far, vector)
    cols = pl.ds(pl.multiple_of((1 - core) * width, width), width)
    for k in range(terms):
        source, weight = term_of(plan, sectors, terms, k)
        product = jnp.dot(lefts[k, :, cols], vector[source], preferred_element_type=jnp.float32)
        product = (partial[k] + product) * weight
        mixed[:, k * width : (k + 1) * width] = product.astype(jnp.bfloat16)
    total[...] = collect(mixed[...], rights)
    extra_shape = (EXTRA_ROWS, kept_ref.shape[2])
    lane = lax.broadcasted_iota(jnp.int32, extra_shape, 1)
    zeros = jnp.zeros(extra_shape, jnp.float32)
    own_sums, z_sums = zeros, zeros
    for k, value in enumerate((0.5 * square_ref[0, 0], sums_ref[0, 0, 0], sums_ref[1, 0, 0])):
        value = jnp.broadcast_to(value, extra_shape)
        own_sums = jnp.where(lane == k, value, own_sums)
        for level in range(3):
            piece = value.astype(jnp.bfloat16).astype(jnp.float32)
            z_sums = jnp.where(lane == 9 * core + 3 * k + level, piece, z_sums)
            value = value - piece

    def packed(top, bottom):
        halves = [
            jnp.concatenate([top[:, col : col + tile], bottom[:, col : col + tile]], axis=1)
            for col in (0, tile)
        ]
        return jnp.where(core == 0, halves[0], halves[1]), jnp.where(core == 0, halves[1], halves[0])

    for k, z_row in enumerate((z, 1 - z)):
        image = []
        for lower in range(2):
            piece = 2 * (x ^ lower)
            image.append(jnp.where(z_row == core, near[piece, 0], far[piece, 0]).astype(jnp.float32))
        tiles_ref[k] = packed(*image)[0].astype(tiles_ref.dtype)
    for xr in range(2):
        for zr in range(2):
            at = (
                pl.ds(pl.multiple_of((z ^ zr) * tile, tile), tile),
                pl.ds(pl.multiple_of((x ^ xr) * width, width), width),
            )
            block = total[at]
            mine, other = packed(block[:half], block[half:])
            kept_ref[2 * zr + xr, :half] = mine
            sent_ref[2 * zr + xr, :half] = other
    for to in range(4):
        kept_ref[to, half:] = (own_sums, zeros, z_sums, zeros)[to]
        sent_ref[to, half:] = (own_sums, zeros, z_sums, zeros)[to]


def last_kernel(plan, own_ref, from_x, from_z, from_xz, tiles_ref, got_ref, first_ref, out_ref):
    _, rows, cols = out_ref.shape
    half = rows // 2
    core, x, y, z, sector = plan[0], plan[1], plan[2], plan[3], plan[4]
    total = own_ref[:half] + from_x[:half].astype(jnp.float32)
    total += from_z[:half].astype(jnp.float32) + from_xz[:half].astype(jnp.float32)
    own_sums = own_ref[half : half + 8]
    z_sums = from_z[half : half + EXTRA_ROWS].astype(jnp.float32)[:8]
    image = jnp.where(x == z, tiles_ref[0], got_ref[...]).astype(jnp.float32)
    lane = lax.broadcasted_iota(jnp.int32, own_sums.shape, 1)

    def pick(values, wanted):
        return jnp.sum(jnp.where(wanted, values, 0.0), axis=1, keepdims=True)[:1]

    sums = []
    for k in range(3):
        z_part = pick(z_sums, (lane % 9 // 3 == k) & (lane < 18))
        sums.append(pick(own_sums, lane == k) + z_part)
    square, inner, norm = sums
    quotient = inner / square
    residual_square = jnp.maximum(norm - quotient * inner, 0.0)
    scale = lax.rsqrt(residual_square / square + EPSILON)
    sizes = plan[PLAN_BITS + 2 * sector], plan[PLAN_BITS + 2 * sector + 1]
    second = (total - quotient * image) * scale
    for k in range(2):
        at = slice(k * half, (k + 1) * half)
        part = slice(k * cols, (k + 1) * cols)
        first_ref[0, at] = image[:, part].astype(jnp.bfloat16)
        row = (2 * z + y) * rows + k * half
        keep = live_block(sizes, row, (2 * x + core) * cols, (half, cols))
        out_ref[0, at] = jnp.where(keep, second[:, part], 0.0).astype(jnp.bfloat16)


def on_device(
    wavefunction, left_environment, right_environment, sector_sizes, pairing, term_mask, coupling
):
    tile = wavefunction.shape[1]
    terms = left_environment.shape[0]
    sectors = lax.axis_size("sec") // SECTOR_BIT
    capacity = tile * GRID_ROWS
    bf16, f32 = jnp.bfloat16, jnp.float32

    def shaped(*shape, dtype=bf16):
        return jax.ShapeDtypeStruct(shape, dtype)

    index = lax.axis_index("sec").astype(jnp.int32)
    bits = [index % 2, index // XBIT % 2, index // YBIT % 2, index // ZBIT % 2, index // SECTOR_BIT]
    sizes = jnp.stack([sector_sizes[0], jnp.take(sector_sizes[1], pairing)], axis=1)
    group = index % GRID_COLS * terms

    def mine(table):
        row = lax.dynamic_slice(table, (bits[4], group), (1, terms))
        return row.reshape(terms)

    plan = jnp.concatenate([jnp.stack(bits), sizes.reshape(-1), mine(coupling), mine(term_mask)])

    start_tile = jnp.concatenate([wavefunction[0, : tile // 2], wavefunction[0, tile // 2 :]], axis=1)
    early = terms // 6
    tiles = [spread(start_tile, flip) for flip in range(0, lax.axis_size("sec"), SECTOR_BIT)]
    gated, tiles[0] = lax.optimization_barrier((left_environment, tiles[0]))
    tiles = jnp.stack(tiles)
    tiles = jnp.stack([tiles, exchange(tiles, YBIT)])
    right_early = exchange(right_environment[:early], YBIT)
    tiles, right_early = lax.optimization_barrier((tiles, right_early))
    tiles = jnp.stack([tiles, exchange(tiles, XBIT)])
    far_tiles = exchange(tiles, CORE)

    left_peer = exchange(gated, ZBIT)
    right_late = exchange(right_environment[early:], YBIT)

    def work(macs):
        return pl.CostEstimate(flops=int(2 * macs), bytes_accessed=terms * tile * capacity * 4, transcendentals=0)

    width = 2 * tile
    macs = terms * tile * capacity * width
    vector_shape = (sectors, capacity, width)
    unit = (4, tile // 2, width)

    def params(mib):
        return pltpu.CompilerParams(vmem_limit_bytes=mib * MIB)

    total_shape = shaped(tile, capacity, dtype=f32)
    mixed_shape = shaped(2, tile, terms * tile)
    start_vector, mixed_own, total_own, square, left_own, right_own = pl.pallas_call(
        lambda *refs: start_kernel(sectors, *refs),
        out_shape=[
            shaped(*vector_shape),
            mixed_shape,
            total_shape,
            shaped(8, 128, dtype=f32),
            shaped(terms, tile, capacity),
            shaped(terms, tile, capacity),
        ],
        in_specs=[smem(), vmem(), vmem(), anywhere(), anywhere(), vmem()],
        out_specs=[vmem()] * 6,
        scratch_shapes=[pltpu.SemaphoreType.DMA((2,))],
        compiler_params=params(16),
        cost_estimate=work(START_COST * macs),
    )(plan, tiles, far_tiles, left_environment, right_environment, right_early)
    mixed_peer, total_peer, lefts = pl.pallas_call(
        lambda *refs: peer_kernel(sectors, *refs),
        out_shape=[mixed_shape, total_shape, shaped(terms, width, capacity)],
        in_specs=[smem()] + [vmem()] * 5,
        out_specs=[vmem()] * 3,
        scratch_shapes=[pltpu.SemaphoreType.DMA((2,))],
        compiler_params=params(PEER_MIB),
        cost_estimate=work(PEER_COST * macs),
    )(plan, start_vector, left_own, left_peer, right_own, right_early)
    late_shape = shaped(terms - early, tile, capacity)
    sent, right_late = pl.pallas_call(
        sent_kernel,
        out_shape=[shaped(*unit, dtype=f32), late_shape],
        in_specs=[smem()] + [vmem()] * 5,
        out_specs=[vmem()] * 2,
        scratch_shapes=[pltpu.VMEM((tile, capacity), f32), pltpu.SemaphoreType.DMA],
        compiler_params=params(16),
        cost_estimate=work(macs),
    )(plan, mixed_own, mixed_peer, total_own, total_peer, right_late)
    kept, rights = pl.pallas_call(
        kept_kernel,
        out_shape=[shaped(*unit, dtype=f32), shaped(terms, width, capacity)],
        in_specs=[smem()] + [vmem()] * 7,
        out_specs=[vmem()] * 2,
        scratch_shapes=[pltpu.VMEM((tile, capacity), f32), pltpu.SemaphoreType.DMA((3,))],
        compiler_params=params(16),
        cost_estimate=work(macs),
    )(plan, mixed_own, mixed_peer, total_own, total_peer, right_own, right_early, right_late)

    summed = kept + exchange(sent, CORE)
    image_unit = (
        summed[0]
        + exchange(summed[1].astype(bf16), XBIT).astype(f32)
        + exchange(summed[2].astype(bf16), ZBIT).astype(f32)
        + exchange(summed[3].astype(bf16), XBIT | ZBIT).astype(f32)
    )
    own_unit = image_unit.astype(bf16)[None]
    gathered = own_unit
    flip = SECTOR_BIT
    while flip < lax.axis_size("sec"):
        gathered = jnp.concatenate([gathered, exchange(gathered, flip)])
        flip *= 2
    units = [gathered]
    for way in (YBIT, XBIT, XBIT | YBIT):
        parts = [exchange(own_unit, way)]
        if sectors > 1:
            parts.append(exchange(gathered[1:], way))
        units.append(jnp.concatenate(parts))
    units = jnp.stack(units)
    far_units = exchange(units, CORE)
    half = tile // 2
    part = (4, half + EXTRA_ROWS, width)
    near_shape = (sectors, width, width)
    partial, sums = pl.pallas_call(
        lambda *refs: near_kernel(sectors, *refs),
        out_shape=[shaped(terms, width, width, dtype=f32), shaped(2, 8, 128, dtype=f32)],
        in_specs=[smem()] + [vmem()] * 3,
        out_specs=[vmem()] * 2,
        scratch_shapes=[pltpu.VMEM(near_shape, bf16)],
        compiler_params=params(20),
        cost_estimate=work(macs),
    )(plan, start_vector, units, lefts)
    kept, sent, image_tiles = pl.pallas_call(
        lambda *refs: second_kernel(sectors, *refs),
        out_shape=[shaped(*part, dtype=f32)] * 2 + [shaped(2, half, width)],
        in_specs=[smem()] + [vmem()] * 7,
        out_specs=[vmem()] * 3,
        scratch_shapes=[
            pltpu.VMEM(near_shape, bf16),
            pltpu.VMEM((width, terms * width), bf16),
            pltpu.VMEM((width, capacity), f32),
        ],
        compiler_params=params(24),
        cost_estimate=work(3 * macs),
    )(plan, square, sums, partial, units, far_units, lefts, rights)
    got_tile = exchange(image_tiles[1], ZBIT)
    summed = kept + exchange(sent, CORE)
    first, second = pl.pallas_call(
        last_kernel,
        out_shape=[shaped(1, tile, tile)] * 2,
        in_specs=[smem()] + [vmem()] * 6,
        out_specs=[vmem()] * 2,
        compiler_params=params(4),
    )(
        plan,
        summed[0],
        exchange(summed[1, :half].astype(bf16), XBIT),
        exchange(summed[2].astype(bf16), ZBIT),
        exchange(summed[3, :half].astype(bf16), XBIT | ZBIT),
        image_tiles,
        got_tile,
    )
    return first, second


def solution(mesh):
    return jax.shard_map(
        on_device,
        mesh=mesh,
        in_specs=(
            P(("groups", "sec"), None, None),
            P(("groups", "sec"), None, None),
            P(("groups", "sec"), None, None),
            P(None, "groups"),
            P("groups"),
            P("groups", None),
            P("groups", None),
        ),
        out_specs=(P(("groups", "sec"), None, None), P(("groups", "sec"), None, None)),
        check_vma=False,
    )
```
